256 devices in a mesh: res: 8 (over z_hi, x), dom: 32 (over z_lo, y, core).
Axes of the slice: x: 4, y: 4, z: 8 (z_hi: 2, z_lo: 4; z = z_hi * 4 + z_lo), core: 2. Of those that a mesh axis runs over, the one named last changes fastest.
Arguments:
- rhs_panel: float32 [8, 48, 8, 1024, 128], P('res', None, None, 'dom'), may hold values from -6 to 6
- inv_diag: float32 [8, 3, 3, 8, 1024, 128], P('res', None, None, None, 'dom'), may hold values from -0.04 to 0.15, as said below
- trans: float32 [8, 3, 8, 1024, 128], P('res', None, None, 'dom'), may hold values from 0.3 to 1.5
- perf_cell: int32 [8, 8192], P('res', 'dom'), may hold values from 0 to 32767
- perf_well: int32 [8, 8192], P('res', 'dom'), may hold values from 0 to 255
- perf_coef: float32 [8, 3, 8192], P('res', None, 'dom'), may hold values from -8 to 8
- perf_count: int32 [8, 32], P('res', 'dom'), may hold values from 32 to 256, as said below
- well_node: int32 [8, 256], P('res'), may hold values from 0 to 2047
- net_block: float32 [16, 2048], replicated, may hold values from -6 to 6
- net_residual: float32 [2048], replicated, may hold values from -6 to 6
Outputs:
- correction: float32 [8, 3, 8, 1024, 128], P('res', None, None, 'dom')
- schur_panel: float32 [16, 2048], replicated
The draws below stay inside these ranges and needn't reach their ends.
Inputs may be any that keep to these rules, and one draw needn't show every extreme that they name: `perf_count`: slots below a device's count are live, the rest are ignored; in every reservoir some device has all 256 slots live. `inv_diag`: diagonal entries positive.
All inputs are finite; a program needn't handle non-finite values.
Results may differ from the reference program's by a relative error of at most 0.00015.
Values sent between devices are 32-bit elements; how exact they have to be, the bound alone decides.
A program may use at most 128 MiB of HBM per device.

```python
import math
import jax
import jax.numpy as jnp
from jax import lax

COLS = 16
NET = 2048
WELLS = 256
SWEEPS = 4
LZ = 8
NY = 128
CX = 32
PERF_DEV = 256
RESERVOIRS = 8
NX = 1024
PERFS = 8192
CELLS_DEV = 32768
N_DOM = 32


def draw_inv_diag(key, part):
    first, second = jax.random.split(key, 2)
    shape = (RESERVOIRS, 3, 3, LZ, NX, NY)
    diagonal = jnp.exp(jax.random.uniform(first, shape, jnp.float32, jnp.log(0.05), jnp.log(0.15)))
    offdiag = jax.random.uniform(second, shape, jnp.float32, -0.03, 0.03)
    identity = jnp.eye(3, dtype=jnp.float32)[None, :, :, None, None, None]
    return jnp.where(identity > 0, diagonal, offdiag).astype(jnp.float32)


def draw_perf_count(key, part):
    first, second, third = jax.random.split(key, 3)
    lighter = jax.random.randint(first, (RESERVOIRS, N_DOM), PERF_DEV // 8, PERF_DEV // 2 + 1)
    heavy = jax.random.randint(second, (RESERVOIRS, N_DOM), 0, 4) == 0
    chosen = jax.random.randint(third, (RESERVOIRS, 1), 0, N_DOM)
    heavy = heavy | (jnp.arange(N_DOM, dtype=jnp.int32)[None, :] == chosen)
    return jnp.where(heavy, PERF_DEV, lighter).astype(jnp.int32)


def plant(values, rng, low, largest):
    spot = [jax.random.randint(jax.random.fold_in(rng, axis), (), 0, length) for axis, length in enumerate(values.shape)]
    longest = values.shape.index(max(values.shape))
    next_to = spot[:longest] + [(spot[longest] + 1) % values.shape[longest]] + spot[longest + 1:]
    return values.at[tuple(spot)].set(low).at[tuple(next_to)].set(largest)


def block_scale(key, shape, shards, least, largest):
    level, own = 1.0, jax.random.fold_in(key, 6)
    for dim, parts in shards:
        steps = jnp.exp(jax.random.uniform(jax.random.fold_in(own, dim), (parts,), jnp.float32, least / len(shards), largest / len(shards)))
        level = level * jnp.repeat(steps, shape[dim] // parts).reshape([-1 if axis == dim else 1 for axis in range(len(shape))])
    return level


def normal_values(stream_key, dims, spread, bound, cuts=(), kind=jnp.bfloat16):
    gain = block_scale(stream_key, dims, cuts, -0.22, 0.18) if cuts else 1.0
    array = jax.random.normal(stream_key, dims, jnp.float32) * spread * gain
    return jnp.minimum(jnp.maximum(array, -bound), bound).astype(kind)


def setup_inputs(seed: int = 0) -> dict:
    seeds = jax.random.split(jax.random.key(seed), 11)
    rhs_panel = normal_values(seeds[0], (RESERVOIRS, 3 * COLS, LZ, NX, NY), 1.0, 6.0, ((0, 8), (3, 32)), jnp.float32)
    inv_diag = draw_inv_diag(jax.random.fold_in(seeds[10], 71), 0)
    trans = jnp.clip(jnp.exp(math.log(1.5) - 1.60943787 * jax.random.uniform(seeds[2], (RESERVOIRS, 3, LZ, NX, NY), jnp.float32) ** block_scale(seeds[2], (RESERVOIRS, 3, LZ, NX, NY), ((0, 8), (3, 32)), -0.2, 0.2)), 0.3, 1.5)
    perf_cell = plant(jax.random.randint(seeds[3], (RESERVOIRS, PERFS), 0, CELLS_DEV), jax.random.fold_in(seeds[3], 1), 0, CELLS_DEV - 1).astype(jnp.int32)
    perf_well = plant(jax.random.randint(seeds[4], (RESERVOIRS, PERFS), 0, WELLS), jax.random.fold_in(seeds[4], 1), 0, WELLS - 1).astype(jnp.int32)
    perf_coef = normal_values(seeds[5], (RESERVOIRS, 3, PERFS), 2.0, 8.0, ((0, 8), (2, 32)), jnp.float32)
    perf_count = draw_perf_count(jax.random.fold_in(seeds[10], 71), 0)
    well_node = plant(jax.random.randint(seeds[7], (RESERVOIRS, WELLS), 0, NET), jax.random.fold_in(seeds[7], 1), 0, NET - 1).astype(jnp.int32)
    net_block = normal_values(seeds[8], (COLS, NET), 1.0, 6.0, (), jnp.float32)
    net_residual = normal_values(seeds[9], (NET,), 1.0, 6.0, (), jnp.float32)
    return {"rhs_panel": rhs_panel, "inv_diag": inv_diag, "trans": trans, "perf_cell": perf_cell, "perf_well": perf_well, "perf_coef": perf_coef, "perf_count": perf_count, "well_node": well_node, "net_block": net_block, "net_residual": net_residual}


HIGH = lax.Precision.HIGHEST

def apply_inverse(inverse, panel_now):
    pieces = panel_now.reshape((3, -1) + panel_now.shape[1:])
    result = []
    for comp in range(3):
        result.append(inverse[comp, 0][None] * pieces[0] + inverse[comp, 1][None] * pieces[1] + inverse[comp, 2][None] * pieces[2])
    return jnp.stack(result).reshape(panel_now.shape)

def coupled(panel_now, x_padded, face_x, face_x_next, face_y, face_z):
    face_y_next = jnp.pad(face_y[:, :, 1:], ((0, 0), (0, 0), (0, 1)))
    face_z_next = jnp.pad(face_z[1:], ((0, 1), (0, 0), (0, 0)))
    y_padded = jnp.pad(panel_now, ((0, 0), (0, 0), (0, 0), (1, 1)))
    z_padded = jnp.pad(panel_now, ((0, 0), (1, 1), (0, 0), (0, 0)))
    summed = face_x * x_padded[:, :, :-2] + face_x_next * x_padded[:, :, 2:]
    summed = summed + face_y * y_padded[..., :-2] + face_y_next * y_padded[..., 2:]
    summed = summed + face_z * z_padded[:, :-2] + face_z_next * z_padded[:, 2:]
    return summed

def reference(rhs_panel, inv_diag, trans, perf_cell, perf_well, perf_coef, perf_count, well_node, net_block, net_residual):
    cols = rhs_panel.shape[1] // 3
    node_ids = jnp.arange(NET, dtype=jnp.int32)
    well_ids = jnp.arange(WELLS, dtype=jnp.int32)
    coupling = jnp.zeros((cols, NET), jnp.float32)
    panels = []
    for reservoir in range(RESERVOIRS):
        source = rhs_panel[reservoir]
        inverse = inv_diag[reservoir]
        face_x = trans[reservoir, 0]
        face_y = trans[reservoir, 1]
        face_z = trans[reservoir, 2]
        face_x_next = jnp.pad(face_x[:, 1:], ((0, 0), (0, 1), (0, 0)))
        panel_now = apply_inverse(inverse, source)
        for sweep_index in range(SWEEPS):
            x_padded = jnp.pad(panel_now, ((0, 0), (0, 0), (1, 1), (0, 0)))
            panel_now = apply_inverse(inverse, source + coupled(panel_now, x_padded, face_x, face_x_next, face_y, face_z))
        slot_index = jnp.arange(PERFS, dtype=jnp.int32)
        device_of = (slot_index // PERF_DEV).astype(jnp.int32)
        cell_index = perf_cell[reservoir]
        layer_at = cell_index // (CX * NY)
        col_at = cell_index // NY % CX + device_of * CX
        row_at = cell_index % NY
        picked = panel_now[:, layer_at, col_at, row_at].reshape(3, cols, PERFS)
        coeffs = perf_coef[reservoir]
        weighted = coeffs[0][None] * picked[0] + coeffs[1][None] * picked[1] + coeffs[2][None] * picked[2]
        live_slots = slot_index % PERF_DEV < perf_count[reservoir][device_of]
        well_onehot = jnp.where((perf_well[reservoir][:, None] == well_ids[None, :]) & live_slots[:, None], 1.0, 0.0).astype(jnp.float32)
        well_rows = jnp.dot(weighted, well_onehot, precision=HIGH)
        node_onehot = jnp.where(well_node[reservoir][:, None] == node_ids[None, :], 1.0, 0.0).astype(jnp.float32)
        coupling = coupling + jnp.dot(well_rows, node_onehot, precision=HIGH)
        panels.append(panel_now)
    schur_panel = net_block - coupling
    weights = jnp.dot(schur_panel, net_residual, precision=HIGH) / math.sqrt(NET)
    fields = []
    for panel_done in panels:
        fields.append(jnp.einsum('ajlcy,j->alcy', panel_done.reshape(3, cols, LZ, NX, NY), weights, precision=HIGH))
    return (jnp.stack(fields), schur_panel)
```

```python
import functools
import math

import jax
import jax.numpy as jnp
from jax import lax
from jax.experimental import pallas as pl
from jax.experimental.pallas import tpu as pltpu
from jax.sharding import PartitionSpec as P

MESH = pl.DeviceIdType.MESH
SWEEPS = 4
COLS, LZ, CX, NY, NET, WELLS, SLOTS = 16, 8, 32, 128, 2048, 256, 256
RES, DOM = 8, 32
GROUPS = 4
GC = COLS // GROUPS
LOW, FIRST, LAST, HIGH = 7, 8, 39, 40
ROWS = 48
BLOCKS = COLS * 3 * LZ
GB = BLOCKS // GROUPS
PIECES = 3


def kernel(
    rhs, inv, trans, cell, well, coef, count, node, net, resid,
    corr_out, schur_out,
    q0, qa, qb, inv_v, trans_v, scale, edge, txm, txp, tym, typ, mats,
    cell_s, well_s, coef_s, count_s, nodes, net_v, resid_v,
    rows, parts, every, hot, lhs, wcol, corr_v,
    in_sem, rhs_sem, halo_send, halo_recv, edge_send, edge_recv,
    node_send, node_recv, rs_send, rs_recv, ga_send, ga_recv, gb_send, gb_recv, out_sem,
):
    f32 = jnp.float32
    res, dom = lax.axis_index("res"), lax.axis_index("dom")
    zlo, yc = dom // 8, dom % 8
    has_left, has_right = dom > 0, dom < DOM - 1

    def local(src, dst, i):
        return pltpu.make_async_copy(src, dst, in_sem.at[i])

    c_trans = local(trans, trans_v, 0)
    c_inv = local(inv, inv_v, 1)
    c_node = local(node, nodes.at[pl.ds(res, 1)], 2)
    c_small = [
        local(cell, cell_s, 3),
        local(well, well_s, 4),
        local(coef, coef_s, 5),
        local(count, count_s, 6),
        local(net, net_v, 7),
        local(resid, resid_v, 8),
    ]
    c_trans.start()
    c_node.start()
    c_inv.start()

    @pl.loop(0, COLS)
    def _(j):
        for c in range(3):
            pltpu.make_async_copy(
                rhs.at[pl.ds((c * COLS + j) * LZ, LZ)],
                q0.at[pl.ds((j * 3 + c) * LZ, LZ), pl.ds(FIRST, CX), :],
                rhs_sem.at[j // GC],
            ).start()

    for copy in c_small:
        copy.start()

    barrier = pltpu.get_barrier_semaphore()

    @pl.loop(1, DOM)
    def _(i):
        pl.semaphore_signal(
            barrier, inc=1, device_id={"dom": lax.rem(dom + i, DOM)}, device_id_type=MESH
        )

    def peer_a(i):
        there = lax.rem(res * 4 + zlo + i, 32)
        return there // 4, lax.rem(there, 4) * 8 + yc

    @pl.loop(1, RES)
    def _(i):
        for z in range(4):
            pl.semaphore_signal(
                barrier,
                inc=1,
                device_id={"res": lax.rem(res + i, RES), "dom": z * 8 + yc},
                device_id_type=MESH,
            )

    lane = lax.broadcasted_iota(jnp.int32, (8, NY), 1)

    c_trans.wait()

    @pl.loop(0, CX // 8)
    def _(xt):
        at = pl.ds(xt * 8, 8)
        own = pl.ds(xt * 8 + FIRST, 8)
        e = jnp.ones((8, NY), f32)
        for l in range(LZ):
            if l:
                e = 1.0 / (trans_v[16 + l, at, :] * e)
            scale[l, own, :] = e
            edge[l, own, :] = trans_v[l, at, :] * e
            ty = trans_v[8 + l, at, :]
            tym[l, at, :] = jnp.where(lane == 0, 0.0, ty * e * pltpu.roll(e, 1, axis=1))
            typ[l, at, :] = jnp.where(lane == NY - 1, 0.0, e * pltpu.roll(ty * e, NY - 1, axis=1))

    @pl.when(jnp.logical_not(has_left))
    def _():
        scale[:, LOW : LOW + 1, :] = jnp.zeros((LZ, 1, NY), f32)
        for buf in (q0, qa, qb):

            @pl.loop(0, BLOCKS)
            def _(b):
                buf[b, LOW : LOW + 1, :] = jnp.zeros((1, NY), f32)

    @pl.when(jnp.logical_not(has_right))
    def _():
        edge[:, HIGH : HIGH + 1, :] = jnp.zeros((LZ, 1, NY), f32)
        for buf in (q0, qa, qb):

            @pl.loop(0, BLOCKS)
            def _(b):
                buf[b, HIGH : HIGH + 1, :] = jnp.zeros((1, NY), f32)

    c_node.wait()
    pl.semaphore_wait(barrier, DOM - 1 + 4 * (RES - 1))

    def remote(src, dst, send, recv, **where):
        return pltpu.make_async_remote_copy(
            src_ref=src, dst_ref=dst, send_sem=send, recv_sem=recv, device_id=where,
            device_id_type=MESH,
        )

    to_right = remote(
        scale.at[:, LAST, :], scale.at[:, LOW, :], edge_send.at[0], edge_recv.at[0],
        dom=jnp.minimum(dom + 1, DOM - 1),
    )
    to_left = remote(
        edge.at[:, FIRST, :], edge.at[:, HIGH, :], edge_send.at[1], edge_recv.at[1],
        dom=jnp.maximum(dom - 1, 0),
    )
    pl.when(has_right)(to_right.start)
    pl.when(has_left)(to_left.start)

    def node_copy(i):
        return remote(
            nodes.at[pl.ds(res, 1)], nodes.at[pl.ds(res, 1)], node_send.at[i], node_recv.at[i],
            res=lax.rem(res + i, RES),
        )

    @pl.loop(1, RES)
    def _(i):
        node_copy(i).start()

    def halo(buf, k, g, side):
        at = pl.ds(g * GB, GB)
        if side == 0:
            return remote(
                buf.at[at, LAST, :], buf.at[at, LOW, :], halo_send.at[k, g, 0],
                halo_recv.at[k, g, 0], dom=jnp.minimum(dom + 1, DOM - 1),
            )
        return remote(
            buf.at[at, FIRST, :], buf.at[at, HIGH, :], halo_send.at[k, g, 1],
            halo_recv.at[k, g, 1], dom=jnp.maximum(dom - 1, 0),
        )

    def halo_start(buf, k, g):
        pl.when(has_right)(halo(buf, k, g, 0).start)
        pl.when(has_left)(halo(buf, k, g, 1).start)

    def halo_wait(buf, k, g):
        @pl.when(has_right)
        def _():
            halo(buf, k, g, 0).wait_send()
            halo(buf, k, g, 1).wait_recv()

        @pl.when(has_left)
        def _():
            halo(buf, k, g, 1).wait_send()
            halo(buf, k, g, 0).wait_recv()

    c_inv.wait()

    @pl.loop(0, GROUPS)
    def _(g):
        whole = q0.at[pl.ds(g * GB, GB), pl.ds(FIRST, CX), :]
        pltpu.make_async_copy(whole, whole, rhs_sem.at[g]).wait()

        @pl.loop(0, LZ * (CX // 8))
        def _(t):
            l, xt = t // 4, lax.rem(t, 4)
            at = pl.ds(xt * 8, 8)
            own = pl.ds(xt * 8 + FIRST, 8)
            back = 1.0 / scale[l, own, :]
            mat = [inv_v[n * LZ + l, at, :] * back for n in range(9)]

            @pl.when(g == 0)
            def _():
                for n in range(9):
                    mats[n * LZ + l, at, :] = mat[n] * back

            for j in range(GC):
                base = (g * GC + j) * 3 * LZ + l
                r = [q0[base + c * LZ, own, :] for c in range(3)]
                for c in range(3):
                    q0[base + c * LZ, own, :] = (
                        mat[3 * c] * r[0] + mat[3 * c + 1] * r[1] + mat[3 * c + 2] * r[2]
                    )

        halo_start(q0, 0, g)

    pl.when(has_right)(to_right.wait_send)
    pl.when(has_left)(to_right.wait_recv)
    pl.when(has_left)(to_left.wait_send)
    pl.when(has_right)(to_left.wait_recv)

    @pl.loop(0, LZ * (CX // 8))
    def _(t):
        l, xt = t // 4, lax.rem(t, 4)
        at = pl.ds(xt * 8, 8)
        own = pl.ds(xt * 8 + FIRST, 8)
        txm[l, at, :] = edge[l, own, :] * scale[l, pl.ds(xt * 8 + LOW, 8), :]
        txp[l, at, :] = scale[l, own, :] * edge[l, pl.ds(xt * 8 + FIRST + 1, 8), :]

    def tile(src, dst, g, l, xt, below, above):
        at = pl.ds(xt * 8, 8)
        own = pl.ds(xt * 8 + FIRST, 8)
        xlo = pl.ds(xt * 8 + LOW, 8)
        xhi = pl.ds(xt * 8 + FIRST + 1, 8)
        am, ap, bm, bp = (ref[l, at, :] for ref in (txm, txp, tym, typ))
        mat = [mats[n * LZ + l, at, :] for n in range(9)]
        for j in range(GC):
            base = (g * GC + j) * 3 * LZ + l
            sums = []
            for c in range(3):
                b = base + c * LZ
                mid = src[b, own, :]
                s = am * src[b, xlo, :] + ap * src[b, xhi, :]
                s = s + (bm * pltpu.roll(mid, 1, axis=1) + bp * pltpu.roll(mid, NY - 1, axis=1))
                if below and above:
                    s = s + (src[b - 1, own, :] + src[b + 1, own, :])
                elif below:
                    s = s + src[b - 1, own, :]
                else:
                    s = s + src[b + 1, own, :]
                sums.append(s)
            for c in range(3):
                b = base + c * LZ
                dst[b, own, :] = (q0[b, own, :] + mat[3 * c] * sums[0]) + (
                    mat[3 * c + 1] * sums[1] + mat[3 * c + 2] * sums[2]
                )

    chain = [q0, qa, qb, qa, qb]
    for k in range(SWEEPS):
        src, dst = chain[k], chain[k + 1]

        @pl.loop(0, GROUPS)
        def _(g):
            halo_wait(src, k, g)

            @pl.loop(0, CX // 8)
            def _(xt):
                tile(src, dst, g, 0, xt, False, True)

                @pl.loop(1, LZ - 1)
                def _(l):
                    tile(src, dst, g, l, xt, True, True)

                tile(src, dst, g, LZ - 1, xt, True, False)

            if k < SWEEPS - 1:
                halo_start(dst, k + 1, g)

    panel = chain[SWEEPS]

    for copy in c_small:
        copy.wait()
    flat = panel.reshape(BLOCKS * ROWS, NY)
    lane16 = lax.broadcasted_iota(jnp.int32, (COLS, NY), 1)
    lane1 = lax.broadcasted_iota(jnp.int32, (1, NY), 1)
    live = count_s[0, 0]

    def slot(s, acc):
        at, w = cell_s[0, s], well_s[0, s]
        l, x, y = at // (CX * NY), lax.rem(at // NY, CX), lax.rem(at, NY)
        w = jnp.where(s < live, w, -1)
        line = None
        for c in range(3):
            part = coef_s[c, 0, s] * flat[
                pl.ds((c * LZ + l) * ROWS + FIRST + x, COLS, stride=3 * LZ * ROWS), :
            ]
            line = part if line is None else line + part
        mask = jnp.where(lane1 == y, scale[l, pl.ds(FIRST + x, 1), :], 0.0)
        line = pltpu.roll(line * mask, (w - y) & (NY - 1), axis=1)
        return tuple(
            acc[h] + jnp.where(lane16 == w - h * NY, line, 0.0) for h in range(2)
        )

    acc = lax.fori_loop(0, SLOTS, slot, (jnp.zeros((COLS, NY), f32),) * 2)
    for h in range(2):
        rows[h * COLS : (h + 1) * COLS, :] = acc[h]

    def rs_copy(i):
        there = lax.rem(dom + i, DOM)
        return remote(
            rows.at[pl.ds(there, 1)], parts.at[pl.ds(dom, 1)], rs_send.at[i], rs_recv.at[i],
            dom=there,
        )

    @pl.loop(1, DOM)
    def _(i):
        rs_copy(i).start()

    parts[pl.ds(dom, 1), :] = rows[pl.ds(dom, 1), :]

    @pl.loop(1, RES)
    def _(i):
        node_copy(i).wait()

    sub = lax.broadcasted_iota(jnp.int32, (256, WELLS), 0)
    for r in range(RES):
        ids = nodes[r : r + 1, :]
        hot[:, r * WELLS : (r + 1) * WELLS] = jnp.where((ids & 255) == sub, 1.0, 0.0).astype(
            jnp.bfloat16
        )

    @pl.loop(1, DOM)
    def _(i):
        rs_copy(i).wait()

    mine = res * 4 + zlo
    every[mine, pl.ds(yc, 1), :] = jnp.sum(parts[...], axis=0, keepdims=True)

    def ga_copy(i):
        r, d = peer_a(i)
        one = every.at[mine, pl.ds(yc, 1), :]
        return remote(one, one, ga_send.at[i], ga_recv.at[i], res=r, dom=d)

    @pl.loop(1, 32)
    def _(i):
        ga_copy(i).start()

    @pl.loop(1, 32)
    def _(i):
        ga_copy(i).wait()

    def gb_copy(i):
        some = every.at[:, yc, :]
        return remote(
            some, some, gb_send.at[i], gb_recv.at[i], dom=zlo * 8 + lax.rem(yc + i, 8)
        )

    @pl.loop(1, 8)
    def _(i):
        gb_copy(i).start()

    @pl.loop(1, 8)
    def _(i):
        gb_copy(i).wait()

    for r in range(RES):
        high = nodes[r : r + 1, :] // 256
        w = jnp.concatenate(
            [
                jnp.concatenate([every[4 * r], every[4 * r + 2]], axis=1),
                jnp.concatenate([every[4 * r + 1], every[4 * r + 3]], axis=1),
            ],
            axis=0,
        )
        for part in range(PIECES):
            now = w.astype(jnp.bfloat16).astype(f32)
            w = w - now
            for hi in range(8):
                at = (hi * PIECES + part) * COLS
                lhs[at : at + COLS, r * WELLS : (r + 1) * WELLS] = jnp.where(
                    high == hi, now, 0.0
                ).astype(jnp.bfloat16)
    spread = lax.dot_general(
        lhs[...], hot[...], (((1,), (1,)), ((), ())), preferred_element_type=f32
    )
    weight = jnp.zeros((COLS, 256), f32)
    for hi in range(8):
        total = None
        for part in range(PIECES):
            at = (hi * PIECES + part) * COLS
            now = spread[at : at + COLS]
            total = now if total is None else total + now
        at = slice(hi * 256, (hi + 1) * 256)
        schur = net_v[:, at] - total
        net_v[:, at] = schur
        weight = weight + schur * resid_v[:, at]
    c_schur = pltpu.make_async_copy(net_v, schur_out, out_sem.at[0])
    c_schur.start()
    wcol[...] = jnp.broadcast_to(
        jnp.sum(weight, axis=1, keepdims=True) * (1.0 / math.sqrt(NET)), (COLS, NY)
    )

    weights = [jnp.broadcast_to(wcol[j : j + 1, :], (8, NY)) for j in range(COLS)]

    @pl.loop(0, 3 * LZ)
    def _(b):
        l = lax.rem(b, LZ)
        for xt in range(CX // 8):
            own = pl.ds(xt * 8 + FIRST, 8)
            total = [None, None]
            for j in range(COLS):
                term = weights[j] * panel[j * 3 * LZ + b, own, :]
                total[j % 2] = term if total[j % 2] is None else total[j % 2] + term
            corr_v[b, xt * 8 : xt * 8 + 8, :] = scale[l, own, :] * (total[0] + total[1])

    c_corr = pltpu.make_async_copy(corr_v, corr_out, out_sem.at[1])
    c_corr.start()
    c_schur.wait()
    c_corr.wait()


def local(rhs, inv, trans, cell, well, coef, count, node, net, resid):
    f32 = jnp.float32
    any_space = pl.BlockSpec(memory_space=pl.ANY)
    vmem = lambda *shape: pltpu.VMEM(shape, f32)
    dma = lambda *shape: pltpu.SemaphoreType.DMA(shape)
    corr, schur = pl.pallas_call(
        kernel,
        out_shape=(
            jax.ShapeDtypeStruct((3 * LZ, CX, NY), f32),
            jax.ShapeDtypeStruct((COLS, NET), f32),
        ),
        in_specs=[any_space] * 10,
        out_specs=[any_space] * 2,
        scratch_shapes=[
            vmem(BLOCKS, ROWS, NY), vmem(BLOCKS, ROWS, NY), vmem(BLOCKS, ROWS, NY),
            vmem(9 * LZ, CX, NY), vmem(3 * LZ, CX, NY),
            vmem(LZ, ROWS, NY), vmem(LZ, ROWS, NY),
            vmem(LZ, CX, NY), vmem(LZ, CX, NY), vmem(LZ, CX, NY), vmem(LZ, CX, NY),
            vmem(9 * LZ, CX, NY),
            pltpu.SMEM((1, SLOTS), jnp.int32), pltpu.SMEM((1, SLOTS), jnp.int32),
            pltpu.SMEM((3, 1, SLOTS), f32), pltpu.SMEM((1, 1), jnp.int32),
            pltpu.VMEM((RES, WELLS), jnp.int32), vmem(COLS, NET), vmem(1, NET),
            vmem(32, NY), vmem(32, NY), vmem(32, 8, NY),
            pltpu.VMEM((256, NET), jnp.bfloat16),
            pltpu.VMEM((8 * PIECES * COLS, NET), jnp.bfloat16),
            vmem(COLS, NY), vmem(3 * LZ, CX, NY),
            dma(9), dma(GROUPS),
            dma(SWEEPS, GROUPS, 2), dma(SWEEPS, GROUPS, 2), dma(2), dma(2),
            dma(RES), dma(RES), dma(DOM), dma(DOM), dma(32), dma(32), dma(8), dma(8), dma(2),
        ],
        compiler_params=pltpu.CompilerParams(
            collective_id=0, has_side_effects=True, vmem_limit_bytes=56 * 1024 * 1024
        ),
        cost_estimate=pl.CostEstimate(
            flops=120_000_000, bytes_accessed=8_500_000, transcendentals=0
        ),
    )(
        rhs.reshape(BLOCKS, CX, NY), inv.reshape(9 * LZ, CX, NY), trans.reshape(3 * LZ, CX, NY),
        cell, well, coef.transpose(1, 0, 2), count, node, net, resid.reshape(1, NET),
    )
    return corr.reshape(1, 3, LZ, CX, NY), schur


def solution(mesh):
    return jax.shard_map(
        local,
        mesh=mesh,
        in_specs=(
            P("res", None, None, "dom", None),
            P("res", None, None, None, "dom", None),
            P("res", None, None, "dom", None),
            P("res", "dom"),
            P("res", "dom"),
            P("res", None, "dom"),
            P("res", "dom"),
            P("res", None),
            P(),
            P(),
        ),
        out_specs=(P("res", None, None, "dom", None), P()),
        check_vma=False,
    )
```

```python
import functools
import math

import jax
import jax.numpy as jnp
from jax import lax
from jax.experimental import pallas as pl
from jax.experimental.pallas import tpu as pltpu
from jax.sharding import PartitionSpec as P

MESH = pl.DeviceIdType.MESH
SWEEPS = 4
COLS, LZ, CX, NY, NET, WELLS, SLOTS = 16, 8, 32, 128, 2048, 256, 256
RES, DOM = 8, 32
GROUPS = 4
GC = COLS // GROUPS
LOW, FIRST, LAST, HIGH = 7, 8, 39, 40
ROWS = 48
BLOCKS = COLS * 3 * LZ
GB = BLOCKS // GROUPS
PIECES = 3
PITCH = 3 * COLS + 1


def kernel(
    rhs, inv, trans, cell, well, coef, count, node, net, resid,
    corr_out, schur_out,
    q0, qa, qb, inv_v, trans_v, scale, edge, txm, txp, tym, typ, mats,
    cell_v, well_v, coef_s, count_s, slots_v, slots_s, nodes, net_v, resid_v,
    lines, rows, parts, sums, every, hot, lhs, wcol, corr_v,
    in_sem, rhs_sem, halo_send, halo_recv, edge_send, edge_recv,
    node_send, node_recv, rs_send, rs_recv, ga_send, ga_recv, gb_send, gb_recv,
    out_sem,
):
    f32 = jnp.float32
    res, dom = lax.axis_index("res"), lax.axis_index("dom")
    zlo, yc = dom // 8, dom % 8
    has_left, has_right = dom > 0, dom < DOM - 1

    def local(src, dst, i):
        return pltpu.make_async_copy(src, dst, in_sem.at[i])

    c_trans = local(trans, trans_v, 0)
    c_inv = local(inv, inv_v, 1)
    c_node = local(node, nodes.at[pl.ds(res, 1)], 2)
    c_small = [
        local(cell, cell_v, 3),
        local(well, well_v, 4),
        local(coef, coef_s, 5),
        local(count, count_s, 6),
        local(net, net_v, 7),
        local(resid, resid_v, 8),
    ]
    c_trans.start()
    c_node.start()
    c_inv.start()

    @pl.loop(0, COLS)
    def _(j):
        for c in range(3):
            pltpu.make_async_copy(
                rhs.at[pl.ds((c * COLS + j) * LZ, LZ)],
                q0.at[pl.ds((j * 3 + c) * LZ, LZ), pl.ds(FIRST, CX), :],
                rhs_sem.at[j // GC],
            ).start()

    for copy in c_small:
        copy.start()

    barrier = pltpu.get_barrier_semaphore()

    def greet(**where):
        pl.semaphore_signal(barrier, inc=1, device_id=where, device_id_type=MESH)

    def plane(i):
        return zlo * 8 + lax.rem(yc + i, 8)

    def column(i):
        there = lax.rem(res * 4 + zlo + i, 32)
        return there // 4, lax.rem(there, 4) * 8 + yc

    greet(dom=lax.rem(dom + 1, DOM))
    greet(dom=lax.rem(dom + DOM - 1, DOM))
    for i in range(1, 8):
        greet(dom=plane(i))

    @pl.loop(1, 32)
    def _(i):
        r, d = column(i)
        greet(res=r, dom=d)

    lane = lax.broadcasted_iota(jnp.int32, (8, NY), 1)

    c_trans.wait()

    @pl.loop(0, CX // 8)
    def _(xt):
        at = pl.ds(xt * 8, 8)
        own = pl.ds(xt * 8 + FIRST, 8)
        e = jnp.ones((8, NY), f32)
        for l in range(LZ):
            if l:
                e = 1.0 / (trans_v[16 + l, at, :] * e)
            scale[l, own, :] = e
            edge[l, own, :] = trans_v[l, at, :] * e
            ty = trans_v[8 + l, at, :]
            tym[l, at, :] = jnp.where(lane == 0, 0.0, ty * e * pltpu.roll(e, 1, axis=1))
            typ[l, at, :] = jnp.where(lane == NY - 1, 0.0, e * pltpu.roll(ty * e, NY - 1, axis=1))

    c_node.wait()
    pl.semaphore_wait(barrier, 2 + 7 + 31)

    def remote(src, dst, send, recv, **where):
        return pltpu.make_async_remote_copy(
            src_ref=src, dst_ref=dst, send_sem=send, recv_sem=recv, device_id=where,
            device_id_type=MESH,
        )

    to_right = remote(
        scale.at[:, LAST, :], scale.at[:, LOW, :], edge_send.at[0], edge_recv.at[0],
        dom=jnp.minimum(dom + 1, DOM - 1),
    )
    to_left = remote(
        edge.at[:, FIRST, :], edge.at[:, HIGH, :], edge_send.at[1], edge_recv.at[1],
        dom=jnp.maximum(dom - 1, 0),
    )
    pl.when(has_right)(to_right.start)
    pl.when(has_left)(to_left.start)

    def node_copy(i):
        return remote(
            nodes.at[pl.ds(res, 1)], nodes.at[pl.ds(res, 1)], node_send.at[i], node_recv.at[i],
            res=lax.rem(res + i, RES),
        )

    @pl.loop(1, RES)
    def _(i):
        node_copy(i).start()

    def halo(buf, k, g, side):
        at = pl.ds(g * GB, GB)
        if side == 0:
            return remote(
                buf.at[at, LAST, :], buf.at[at, LOW, :], halo_send.at[k, g, 0],
                halo_recv.at[k, g, 0], dom=jnp.minimum(dom + 1, DOM - 1),
            )
        return remote(
            buf.at[at, FIRST, :], buf.at[at, HIGH, :], halo_send.at[k, g, 1],
            halo_recv.at[k, g, 1], dom=jnp.maximum(dom - 1, 0),
        )

    def halo_start(buf, k, g):
        pl.when(has_right)(halo(buf, k, g, 0).start)
        pl.when(has_left)(halo(buf, k, g, 1).start)

    def halo_wait(buf, k, g):
        @pl.when(has_right)
        def _():
            halo(buf, k, g, 0).wait_send()
            halo(buf, k, g, 1).wait_recv()

        @pl.when(has_left)
        def _():
            halo(buf, k, g, 1).wait_send()
            halo(buf, k, g, 0).wait_recv()

    for copy in c_small:
        copy.wait()
    at, to = cell_v[...], well_v[...]
    number = lax.broadcasted_iota(jnp.int32, (1, SLOTS), 1)
    slots_v[0:1, :] = (at // NY) * PITCH
    slots_v[1:2, :] = (to - at) & (NY - 1)
    slots_v[2:3, :] = jnp.where(number < count_s[0, 0], to, -1)
    c_slots = local(slots_v, slots_s, 9)
    c_slots.start()

    def clear(row, faces):
        faces[:, row : row + 1, :] = jnp.zeros((LZ, 1, NY), f32)

        @pl.loop(0, BLOCKS // 8)
        def _(b):
            for i in range(8):
                for buf in (q0, qa, qb):
                    buf[b * 8 + i, row : row + 1, :] = jnp.zeros((1, NY), f32)

    @pl.when(jnp.logical_not(has_left))
    def _():
        clear(LOW, scale)

    @pl.when(jnp.logical_not(has_right))
    def _():
        clear(HIGH, edge)

    c_inv.wait()

    @pl.loop(0, LZ * (CX // 8))
    def _(t):
        l, xt = t // 4, lax.rem(t, 4)
        at = pl.ds(xt * 8, 8)
        back = 1.0 / scale[l, pl.ds(xt * 8 + FIRST, 8), :]
        for n in range(9):
            mat = inv_v[n * LZ + l, at, :] * back
            inv_v[n * LZ + l, at, :] = mat
            mats[n * LZ + l, at, :] = mat * back

    @pl.loop(0, GROUPS)
    def _(g):
        whole = q0.at[pl.ds(g * GB, GB), pl.ds(FIRST, CX), :]
        pltpu.make_async_copy(whole, whole, rhs_sem.at[g]).wait()

        @pl.loop(0, LZ)
        def _(l):
            for xt in range(CX // 8):
                own = slice(xt * 8 + FIRST, xt * 8 + FIRST + 8)
                mat = [inv_v[n * LZ + l, xt * 8 : xt * 8 + 8, :] for n in range(9)]
                for j in range(GC):
                    base = (g * GC + j) * 3 * LZ + l
                    r = [q0[base + c * LZ, own, :] for c in range(3)]
                    for c in range(3):
                        q0[base + c * LZ, own, :] = (
                            mat[3 * c] * r[0] + mat[3 * c + 1] * r[1] + mat[3 * c + 2] * r[2]
                        )

        halo_start(q0, 0, g)

    pl.when(has_right)(to_right.wait_send)
    pl.when(has_left)(to_right.wait_recv)
    pl.when(has_left)(to_left.wait_send)
    pl.when(has_right)(to_left.wait_recv)

    @pl.loop(0, LZ * (CX // 8))
    def _(t):
        l, xt = t // 4, lax.rem(t, 4)
        at = pl.ds(xt * 8, 8)
        own = pl.ds(xt * 8 + FIRST, 8)
        txm[l, at, :] = edge[l, own, :] * scale[l, pl.ds(xt * 8 + LOW, 8), :]
        txp[l, at, :] = scale[l, own, :] * edge[l, pl.ds(xt * 8 + FIRST + 1, 8), :]

    def tile(src, dst, g, l, xt, below, above, last):
        at = slice(xt * 8, xt * 8 + 8)
        own = slice(xt * 8 + FIRST, xt * 8 + FIRST + 8)
        xlo = slice(xt * 8 + LOW, xt * 8 + LOW + 8)
        xhi = slice(xt * 8 + FIRST + 1, xt * 8 + FIRST + 9)
        am, ap, bm, bp = (ref[l, at, :] for ref in (txm, txp, tym, typ))
        mat = [mats[n * LZ + l, at, :] for n in range(9)]
        for j in range(GC):
            base = (g * GC + j) * 3 * LZ + l
            sums = []
            for c in range(3):
                b = base + c * LZ
                mid = src[b, own, :]
                s = am * src[b, xlo, :] + ap * src[b, xhi, :]
                s = s + (bm * pltpu.roll(mid, 1, axis=1) + bp * pltpu.roll(mid, NY - 1, axis=1))
                if below and above:
                    s = s + (src[b - 1, own, :] + src[b + 1, own, :])
                elif below:
                    s = s + src[b - 1, own, :]
                else:
                    s = s + src[b + 1, own, :]
                sums.append(s)
            for c in range(3):
                b = base + c * LZ
                out = (q0[b, own, :] + mat[3 * c] * sums[0]) + (
                    mat[3 * c + 1] * sums[1] + mat[3 * c + 2] * sums[2]
                )
                if last:
                    out = out * scale[l, own, :]
                    line = (l * CX + xt * 8) * PITCH + c * COLS + g * GC + j
                    lines[pl.ds(line, 8, stride=PITCH), :] = out
                dst[b, own, :] = out

    chain = [q0, qa, qb, qa, qb]
    for k in range(SWEEPS):
        src, dst, last = chain[k], chain[k + 1], k == SWEEPS - 1

        def part(g, columns, src=src, dst=dst, last=last):
            for l in range(LZ):
                for xt in columns:
                    tile(src, dst, g, l, xt, l > 0, l < LZ - 1, last)

        @pl.loop(0, GROUPS)
        def _(g):
            halo_wait(src, k, g)
            part(g, (0, CX // 8 - 1))
            if not last:
                halo_start(dst, k + 1, g)
            part(g, range(1, CX // 8 - 1))

    panel = chain[SWEEPS]

    c_slots.wait()
    lane = lax.broadcasted_iota(jnp.int32, (COLS, NY), 1)

    def slot(s, acc):
        base, turn, w = (slots_s[i, s] for i in range(3))
        line = None
        for c in range(3):
            part = coef_s[c, 0, s] * lines[pl.ds(base + c * COLS, COLS), :]
            line = part if line is None else line + part
        line = pltpu.roll(line, turn, axis=1)
        return tuple(acc[h] + jnp.where(lane == w - h * NY, line, 0.0) for h in range(2))

    acc = lax.fori_loop(0, SLOTS, slot, (jnp.zeros((COLS, NY), f32),) * 2, unroll=8)
    for h in range(2):
        for half in range(2):
            rows[2 * h + half] = acc[h][half * 8 : half * 8 + 8]

    def rs_copy(i):
        there = plane(i)
        return remote(
            rows.at[:, lax.rem(there, 8), :], parts.at[yc, pl.ds(0, 4), :], rs_send.at[i],
            rs_recv.at[i], dom=there,
        )

    @pl.loop(1, 8)
    def _(i):
        rs_copy(i).start()

    for z in range(4):
        parts[yc, z : z + 1, :] = rows[z, pl.ds(yc, 1), :]

    @pl.loop(1, RES)
    def _(i):
        node_copy(i).wait()

    sub = lax.broadcasted_iota(jnp.int32, (256, WELLS), 0)
    for r in range(RES):
        ids = nodes[r : r + 1, :]
        hot[:, r * WELLS : (r + 1) * WELLS] = jnp.where((ids & 255) == sub, 1.0, 0.0).astype(
            jnp.bfloat16
        )

    @pl.loop(1, 8)
    def _(i):
        rs_copy(i).wait()

    total = parts[0, 0:4, :]
    for i in range(1, 8):
        total = total + parts[i, 0:4, :]
    mine = res * 4 + zlo
    sums[mine, 0:4, :] = total

    def ga_copy(i):
        r, d = column(i)
        some = sums.at[mine, pl.ds(0, 4), :]
        return remote(some, some, ga_send.at[i], ga_recv.at[i], res=r, dom=d)

    @pl.loop(1, 32)
    def _(i):
        ga_copy(i).start()

    @pl.loop(1, 32)
    def _(i):
        ga_copy(i).wait()

    for r in range(RES):
        total = (sums[4 * r, 0:4, :] + sums[4 * r + 1, 0:4, :]) + (
            sums[4 * r + 2, 0:4, :] + sums[4 * r + 3, 0:4, :]
        )
        for z in range(4):
            every[4 * r + z, pl.ds(yc, 1), :] = total[z : z + 1]

    def gb_copy(i):
        some = every.at[:, yc, :]
        return remote(
            some, some, gb_send.at[i], gb_recv.at[i], dom=plane(i)
        )

    @pl.loop(1, 8)
    def _(i):
        gb_copy(i).start()

    @pl.loop(1, 8)
    def _(i):
        gb_copy(i).wait()

    for r in range(RES):
        high = nodes[r : r + 1, :] // 256
        w = jnp.concatenate(
            [
                jnp.concatenate([every[4 * r], every[4 * r + 2]], axis=1),
                jnp.concatenate([every[4 * r + 1], every[4 * r + 3]], axis=1),
            ],
            axis=0,
        )
        for part in range(PIECES):
            now = w.astype(jnp.bfloat16).astype(f32)
            w = w - now
            for hi in range(8):
                at = (hi * PIECES + part) * COLS
                lhs[at : at + COLS, r * WELLS : (r + 1) * WELLS] = jnp.where(
                    high == hi, now, 0.0
                ).astype(jnp.bfloat16)
    spread = lax.dot_general(
        lhs[...], hot[...], (((1,), (1,)), ((), ())), preferred_element_type=f32
    )
    weight = jnp.zeros((COLS, 256), f32)
    for hi in range(8):
        total = None
        for part in range(PIECES):
            at = (hi * PIECES + part) * COLS
            now = spread[at : at + COLS]
            total = now if total is None else total + now
        at = slice(hi * 256, (hi + 1) * 256)
        schur = net_v[:, at] - total
        net_v[:, at] = schur
        weight = weight + schur * resid_v[:, at]
    c_schur = pltpu.make_async_copy(net_v, schur_out, out_sem.at[0])
    c_schur.start()
    wcol[...] = jnp.broadcast_to(
        jnp.sum(weight, axis=1, keepdims=True) * (1.0 / math.sqrt(NET)), (COLS, NY)
    )

    weights = [jnp.broadcast_to(wcol[j : j + 1, :], (8, NY)) for j in range(COLS)]

    @pl.loop(0, 3 * LZ)
    def _(b):
        for xt in range(CX // 8):
            own = slice(xt * 8 + FIRST, xt * 8 + FIRST + 8)
            total = [None, None]
            for j in range(COLS):
                term = weights[j] * panel[j * 3 * LZ + b, own, :]
                total[j % 2] = term if total[j % 2] is None else total[j % 2] + term
            corr_v[b, xt * 8 : xt * 8 + 8, :] = total[0] + total[1]

    c_corr = pltpu.make_async_copy(corr_v, corr_out, out_sem.at[1])
    c_corr.start()
    c_schur.wait()
    c_corr.wait()


def hand_over(corr, schur, corr_out, schur_out, corr_v, schur_v, sem_in, sem_out):
    pieces = [(schur, schur_v, schur_out)]
    for i in range(3):
        at = pl.ds(i * LZ, LZ)
        pieces.append((corr.at[at], corr_v.at[at], corr_out.at[at]))
    into = [pltpu.make_async_copy(p[0], p[1], sem_in.at[i]) for i, p in enumerate(pieces)]
    away = [pltpu.make_async_copy(p[1], p[2], sem_out.at[i]) for i, p in enumerate(pieces)]
    for copy in into:
        copy.start()
    for first, then in zip(into, away):
        first.wait()
        then.start()
    for copy in away:
        copy.wait()


def local(rhs, inv, trans, cell, well, coef, count, node, net, resid):
    f32 = jnp.float32
    any_space = pl.BlockSpec(memory_space=pl.ANY)
    vmem = lambda *shape: pltpu.VMEM(shape, f32)
    dma = lambda *shape: pltpu.SemaphoreType.DMA(shape)
    corr, schur = pl.pallas_call(
        kernel,
        out_shape=(
            jax.ShapeDtypeStruct((3 * LZ, CX, NY), f32),
            jax.ShapeDtypeStruct((COLS, NET), f32),
        ),
        in_specs=[any_space] * 10,
        out_specs=[any_space] * 2,
        scratch_shapes=[
            vmem(BLOCKS, ROWS, NY), vmem(BLOCKS, ROWS, NY), vmem(BLOCKS, ROWS, NY),
            vmem(9 * LZ, CX, NY), vmem(3 * LZ, CX, NY),
            vmem(LZ, ROWS, NY), vmem(LZ, ROWS, NY),
            vmem(LZ, CX, NY), vmem(LZ, CX, NY), vmem(LZ, CX, NY), vmem(LZ, CX, NY),
            vmem(9 * LZ, CX, NY),
            pltpu.VMEM((1, SLOTS), jnp.int32), pltpu.VMEM((1, SLOTS), jnp.int32),
            pltpu.SMEM((3, 1, SLOTS), f32), pltpu.SMEM((1, 1), jnp.int32),
            pltpu.VMEM((8, SLOTS), jnp.int32), pltpu.SMEM((8, SLOTS), jnp.int32),
            pltpu.VMEM((RES, WELLS), jnp.int32), vmem(COLS, NET), vmem(1, NET),
            vmem(LZ * CX * PITCH, NY),
            vmem(4, 8, NY), vmem(8, 8, NY), vmem(32, 8, NY), vmem(32, 8, NY),
            pltpu.VMEM((256, NET), jnp.bfloat16),
            pltpu.VMEM((8 * PIECES * COLS, NET), jnp.bfloat16),
            vmem(COLS, NY), vmem(3 * LZ, CX, NY),
            dma(10), dma(GROUPS),
            dma(SWEEPS, GROUPS, 2), dma(SWEEPS, GROUPS, 2), dma(2), dma(2),
            dma(RES), dma(RES), dma(8), dma(8), dma(32), dma(32), dma(8), dma(8), dma(2),
        ],
        compiler_params=pltpu.CompilerParams(
            collective_id=0, has_side_effects=True, vmem_limit_bytes=56 * 1024 * 1024
        ),
        cost_estimate=pl.CostEstimate(
            flops=120_000_000, bytes_accessed=8_500_000, transcendentals=0
        ),
    )(
        rhs.reshape(BLOCKS, CX, NY), inv.reshape(9 * LZ, CX, NY), trans.reshape(3 * LZ, CX, NY),
        cell, well, coef.transpose(1, 0, 2), count, node, net, resid.reshape(1, NET),
    )
    corr, schur = pl.pallas_call(
        hand_over,
        out_shape=(
            jax.ShapeDtypeStruct((3 * LZ, CX, NY), f32),
            jax.ShapeDtypeStruct((COLS, NET), f32),
        ),
        in_specs=[any_space] * 2,
        out_specs=[any_space] * 2,
        scratch_shapes=[vmem(3 * LZ, CX, NY), vmem(COLS, NET), dma(4), dma(4)],
    )(corr, schur)
    return corr.reshape(1, 3, LZ, CX, NY), schur


def solution(mesh):
    return jax.shard_map(
        local,
        mesh=mesh,
        in_specs=(
            P("res", None, None, "dom", None),
            P("res", None, None, None, "dom", None),
            P("res", None, None, "dom", None),
            P("res", "dom"),
            P("res", "dom"),
            P("res", None, "dom"),
            P("res", "dom"),
            P("res", None),
            P(),
            P(),
        ),
        out_specs=(P("res", None, None, "dom", None), P()),
        check_vma=False,
    )
```

```python
import functools
import math

import jax
import jax.numpy as jnp
from jax import lax
from jax.experimental import pallas as pl
from jax.experimental.pallas import tpu as pltpu
from jax.sharding import PartitionSpec as P

MESH = pl.DeviceIdType.MESH
SWEEPS = 4
COLS, LZ, CX, NY, NET, WELLS, SLOTS = 16, 8, 32, 128, 2048, 256, 256
RES, DOM = 8, 32
GROUPS = 4
GC = COLS // GROUPS
LOW, FIRST, LAST, HIGH = 7, 8, 39, 40
ROWS = 48
BLOCKS = COLS * 3 * LZ
GB = BLOCKS // GROUPS
PIECES = 3
PITCH = 3 * COLS + 1


def kernel(
    rhs, inv, trans, cell, well, coef, count, node, net, resid,
    corr_out, schur_out,
    q0, qa, qb, inv_v, trans_v, scale, edge, txm, txp, tym, typ, mats,
    cell_v, well_v, coef_s, count_s, slots_v, slots_s, nodes, net_v, resid_v,
    lines, rows, parts, sums, hot, lhs, wcol, schur_v,
    in_sem, rhs_sem, halo_send, halo_recv, edge_send, edge_recv,
    node_send, node_recv, rs_send, rs_recv, ga_send, ga_recv, gw_send, gw_recv, gb_send,
    gb_recv,
):
    f32 = jnp.float32
    res, dom = lax.axis_index("res"), lax.axis_index("dom")
    zlo, yc = dom // 8, dom % 8
    has_left, has_right = dom > 0, dom < DOM - 1

    def local(src, dst, i):
        return pltpu.make_async_copy(src, dst, in_sem.at[i])

    c_trans = local(trans, trans_v, 0)
    c_inv = local(inv, inv_v, 1)
    c_node = local(node, nodes.at[pl.ds(res, 1)], 2)
    c_small = [
        local(cell, cell_v, 3),
        local(well, well_v, 4),
        local(coef, coef_s, 5),
        local(count, count_s, 6),
    ]
    c_trans.start()
    c_node.start()
    c_inv.start()

    @pl.loop(0, COLS)
    def _(j):
        for c in range(3):
            pltpu.make_async_copy(
                rhs.at[pl.ds((c * COLS + j) * LZ, LZ)],
                q0.at[pl.ds((j * 3 + c) * LZ, LZ), pl.ds(FIRST, CX), :],
                rhs_sem.at[j // GC],
            ).start()

    for copy in c_small:
        copy.start()
    for hi in range(8):
        at = pl.ds(hi * 256, 256)
        for half in range(2):
            local(
                net.at[pl.ds(half * 8 + yc, 1), at], net_v.at[half, pl.ds(hi, 1), :], 7
            ).start()
        local(resid.at[:, at], resid_v.at[pl.ds(hi, 1), :], 8).start()

    barrier = pltpu.get_barrier_semaphore()

    def greet(**where):
        pl.semaphore_signal(barrier, inc=1, device_id=where, device_id_type=MESH)

    def plane(i):
        return zlo * 8 + lax.rem(yc + i, 8)

    def column(i):
        there = lax.rem(res * 4 + zlo + i, 32)
        return there // 4, lax.rem(there, 4) * 8 + yc

    greet(dom=lax.rem(dom + 1, DOM))
    greet(dom=lax.rem(dom + DOM - 1, DOM))
    for i in range(1, 8):
        greet(dom=plane(i))

    @pl.loop(1, 32)
    def _(i):
        r, d = column(i)
        greet(res=r, dom=d)

    lane = lax.broadcasted_iota(jnp.int32, (8, NY), 1)

    c_trans.wait()

    @pl.loop(0, CX // 8)
    def _(xt):
        at = pl.ds(xt * 8, 8)
        own = pl.ds(xt * 8 + FIRST, 8)
        e = jnp.ones((8, NY), f32)
        for l in range(LZ):
            if l:
                e = 1.0 / (trans_v[16 + l, at, :] * e)
            scale[l, own, :] = e
            edge[l, own, :] = trans_v[l, at, :] * e
            ty = trans_v[8 + l, at, :]
            tym[l, at, :] = jnp.where(lane == 0, 0.0, ty * e * pltpu.roll(e, 1, axis=1))
            typ[l, at, :] = jnp.where(lane == NY - 1, 0.0, e * pltpu.roll(ty * e, NY - 1, axis=1))

    c_node.wait()
    pl.semaphore_wait(barrier, 2 + 7 + 31)

    def remote(src, dst, send, recv, **where):
        return pltpu.make_async_remote_copy(
            src_ref=src, dst_ref=dst, send_sem=send, recv_sem=recv, device_id=where,
            device_id_type=MESH,
        )

    to_right = remote(
        scale.at[:, LAST, :], scale.at[:, LOW, :], edge_send.at[0], edge_recv.at[0],
        dom=jnp.minimum(dom + 1, DOM - 1),
    )
    to_left = remote(
        edge.at[:, FIRST, :], edge.at[:, HIGH, :], edge_send.at[1], edge_recv.at[1],
        dom=jnp.maximum(dom - 1, 0),
    )
    pl.when(has_right)(to_right.start)
    pl.when(has_left)(to_left.start)

    def node_copy(i):
        return remote(
            nodes.at[pl.ds(res, 1)], nodes.at[pl.ds(res, 1)], node_send, node_recv,
            res=lax.rem(res + i, RES),
        )

    @pl.loop(1, RES)
    def _(i):
        node_copy(i).start()

    def halo(buf, k, g, side):
        at = pl.ds(g * GB, GB)
        if side == 0:
            return remote(
                buf.at[at, LAST, :], buf.at[at, LOW, :], halo_send.at[k, g, 0],
                halo_recv.at[k, g, 0], dom=jnp.minimum(dom + 1, DOM - 1),
            )
        return remote(
            buf.at[at, FIRST, :], buf.at[at, HIGH, :], halo_send.at[k, g, 1],
            halo_recv.at[k, g, 1], dom=jnp.maximum(dom - 1, 0),
        )

    def halo_start(buf, k, g):
        pl.when(has_right)(halo(buf, k, g, 0).start)
        pl.when(has_left)(halo(buf, k, g, 1).start)

    def halo_wait(buf, k, g):
        @pl.when(has_right)
        def _():
            halo(buf, k, g, 0).wait_send()
            halo(buf, k, g, 1).wait_recv()

        @pl.when(has_left)
        def _():
            halo(buf, k, g, 1).wait_send()
            halo(buf, k, g, 0).wait_recv()

    for copy in c_small:
        copy.wait()
    at, to = cell_v[...], well_v[...]
    number = lax.broadcasted_iota(jnp.int32, (1, SLOTS), 1)
    slots_v[0:1, :] = (at // NY) * PITCH
    slots_v[1:2, :] = (to - at) & (NY - 1)
    slots_v[2:3, :] = jnp.where(number < count_s[0, 0], to, -1)
    c_slots = local(slots_v, slots_s, 9)
    c_slots.start()

    def clear(row, faces):
        faces[:, row : row + 1, :] = jnp.zeros((LZ, 1, NY), f32)

        @pl.loop(0, BLOCKS // 8)
        def _(b):
            for i in range(8):
                for buf in (q0, qa, qb):
                    buf[b * 8 + i, row : row + 1, :] = jnp.zeros((1, NY), f32)

    @pl.when(jnp.logical_not(has_left))
    def _():
        clear(LOW, scale)

    @pl.when(jnp.logical_not(has_right))
    def _():
        clear(HIGH, edge)

    c_inv.wait()

    @pl.loop(0, LZ * (CX // 8))
    def _(t):
        l, xt = t // 4, lax.rem(t, 4)
        at = pl.ds(xt * 8, 8)
        back = 1.0 / scale[l, pl.ds(xt * 8 + FIRST, 8), :]
        for n in range(9):
            mat = inv_v[n * LZ + l, at, :] * back
            inv_v[n * LZ + l, at, :] = mat
            mats[n * LZ + l, at, :] = mat * back

    @pl.loop(0, GROUPS)
    def _(g):
        whole = q0.at[pl.ds(g * GB, GB), pl.ds(FIRST, CX), :]
        pltpu.make_async_copy(whole, whole, rhs_sem.at[g]).wait()

        @pl.loop(0, LZ)
        def _(l):
            for xt in range(CX // 8):
                own = slice(xt * 8 + FIRST, xt * 8 + FIRST + 8)
                mat = [inv_v[n * LZ + l, xt * 8 : xt * 8 + 8, :] for n in range(9)]
                for j in range(GC):
                    base = (g * GC + j) * 3 * LZ + l
                    r = [q0[base + c * LZ, own, :] for c in range(3)]
                    for c in range(3):
                        q0[base + c * LZ, own, :] = (
                            mat[3 * c] * r[0] + mat[3 * c + 1] * r[1] + mat[3 * c + 2] * r[2]
                        )

        halo_start(q0, 0, g)

    pl.when(has_right)(to_right.wait_send)
    pl.when(has_left)(to_right.wait_recv)
    pl.when(has_left)(to_left.wait_send)
    pl.when(has_right)(to_left.wait_recv)

    @pl.loop(0, LZ * (CX // 8))
    def _(t):
        l, xt = t // 4, lax.rem(t, 4)
        at = pl.ds(xt * 8, 8)
        own = pl.ds(xt * 8 + FIRST, 8)
        txm[l, at, :] = edge[l, own, :] * scale[l, pl.ds(xt * 8 + LOW, 8), :]
        txp[l, at, :] = scale[l, own, :] * edge[l, pl.ds(xt * 8 + FIRST + 1, 8), :]

    def tile(src, dst, g, l, xt, below, above, last):
        at = slice(xt * 8, xt * 8 + 8)
        own = slice(xt * 8 + FIRST, xt * 8 + FIRST + 8)
        xlo = slice(xt * 8 + LOW, xt * 8 + LOW + 8)
        xhi = slice(xt * 8 + FIRST + 1, xt * 8 + FIRST + 9)
        am, ap, bm, bp = (ref[l, at, :] for ref in (txm, txp, tym, typ))
        mat = [mats[n * LZ + l, at, :] for n in range(9)]
        for j in range(GC):
            base = (g * GC + j) * 3 * LZ + l
            sums = []
            for c in range(3):
                b = base + c * LZ
                mid = src[b, own, :]
                s = am * src[b, xlo, :] + ap * src[b, xhi, :]
                s = s + (bm * pltpu.roll(mid, 1, axis=1) + bp * pltpu.roll(mid, NY - 1, axis=1))
                if below and above:
                    s = s + (src[b - 1, own, :] + src[b + 1, own, :])
                elif below:
                    s = s + src[b - 1, own, :]
                else:
                    s = s + src[b + 1, own, :]
                sums.append(s)
            for c in range(3):
                b = base + c * LZ
                out = (q0[b, own, :] + mat[3 * c] * sums[0]) + (
                    mat[3 * c + 1] * sums[1] + mat[3 * c + 2] * sums[2]
                )
                if last:
                    out = out * scale[l, own, :]
                    line = (l * CX + xt * 8) * PITCH + c * COLS + g * GC + j
                    lines[pl.ds(line, 8, stride=PITCH), :] = out
                dst[b, own, :] = out

    chain = [q0, qa, qb, qa, qb]
    for k in range(SWEEPS):
        src, dst, last = chain[k], chain[k + 1], k == SWEEPS - 1

        def part(g, columns, src=src, dst=dst, last=last):
            for l in range(LZ):
                for xt in columns:
                    tile(src, dst, g, l, xt, l > 0, l < LZ - 1, last)

        @pl.loop(0, GROUPS)
        def _(g):
            halo_wait(src, k, g)
            part(g, (0, CX // 8 - 1))
            if not last:
                halo_start(dst, k + 1, g)
            part(g, range(1, CX // 8 - 1))

    panel = chain[SWEEPS]

    c_slots.wait()
    lane = lax.broadcasted_iota(jnp.int32, (COLS, NY), 1)

    def slot(s, acc):
        base, turn, w = (slots_s[i, s] for i in range(3))
        line = None
        for c in range(3):
            part = coef_s[c, 0, s] * lines[pl.ds(base + c * COLS, COLS), :]
            line = part if line is None else line + part
        line = pltpu.roll(line, turn, axis=1)
        return tuple(acc[h] + jnp.where(lane == w - h * NY, line, 0.0) for h in range(2))

    acc = lax.fori_loop(0, SLOTS, slot, (jnp.zeros((COLS, NY), f32),) * 2, unroll=16)
    for h in range(2):
        for half in range(2):
            rows[2 * h + half] = acc[h][half * 8 : half * 8 + 8]

    def rs_copy(i):
        there = plane(i)
        return remote(
            rows.at[:, lax.rem(there, 8), :], parts.at[yc, pl.ds(0, 4), :], rs_send, rs_recv,
            dom=there,
        )

    @pl.loop(1, 8)
    def _(i):
        rs_copy(i).start()

    for z in range(4):
        parts[yc, z : z + 1, :] = rows[z, pl.ds(yc, 1), :]

    def wait_all(ref, *sems):
        for sem in sems:
            pltpu.make_async_copy(ref, ref, sem).wait()

    wait_all(nodes.at[pl.ds(0, RES - 1)], node_send, node_recv)

    sub = lax.broadcasted_iota(jnp.int32, (256, WELLS), 0)
    for r in range(RES):
        ids = nodes[r : r + 1, :]
        hot[:, r * WELLS : (r + 1) * WELLS] = jnp.where((ids & 255) == sub, 1.0, 0.0).astype(
            jnp.bfloat16
        )

    wait_all(parts.at[pl.ds(0, 7), pl.ds(0, 4), :], rs_send, rs_recv)

    total = parts[0, 0:4, :]
    for i in range(1, 8):
        total = total + parts[i, 0:4, :]
    mine = res * 4 + zlo
    sums[mine, 0:4, :] = total

    def ga_copy(i):
        r, d = column(i)
        some = sums.at[mine, pl.ds(0, 4), :]
        return remote(some, some, ga_send, ga_recv, res=r, dom=d)

    @pl.loop(1, 32)
    def _(i):
        ga_copy(i).start()

    wait_all(net_v, in_sem.at[7])
    wait_all(resid_v, in_sem.at[8])
    wait_all(sums.at[pl.ds(0, 31), pl.ds(0, 4), :], ga_send, ga_recv)

    sub8 = lax.broadcasted_iota(jnp.int32, (8, WELLS), 0)
    for r in range(RES):
        w = (sums[4 * r, 0:4, :] + sums[4 * r + 1, 0:4, :]) + (
            sums[4 * r + 2, 0:4, :] + sums[4 * r + 3, 0:4, :]
        )
        here = nodes[r : r + 1, :] // 256 == sub8
        for part in range(PIECES):
            now = w.astype(jnp.bfloat16).astype(f32)
            w = w - now
            tiles = []
            for half in range(2):
                line = jnp.concatenate([now[half : half + 1], now[half + 2 : half + 3]], axis=1)
                tiles.append(jnp.where(here, line, 0.0))
            lhs[part * 16 : part * 16 + 16, r * WELLS : (r + 1) * WELLS] = jnp.concatenate(
                tiles, axis=0
            ).astype(jnp.bfloat16)
    spread = lax.dot_general(
        lhs[...], hot[...], (((1,), (1,)), ((), ())), preferred_element_type=f32
    )
    spread = (spread[0:16] + spread[16:32]) + spread[32:48]
    for half in range(2):
        schur = net_v[half] - spread[half * 8 : half * 8 + 8]
        schur_v[half, yc] = schur
        weight = jnp.sum(schur * resid_v[...], axis=0, keepdims=True)
        weight = jnp.sum(weight, axis=1, keepdims=True) * (1.0 / math.sqrt(NET))
        wcol[half, pl.ds(yc, 1), :] = jnp.broadcast_to(weight, (1, NY))

    def gw_copy(i):
        some = wcol.at[:, yc, :]
        return remote(some, some, gw_send, gw_recv, dom=plane(i))

    def gb_copy(i):
        some = schur_v.at[:, yc]
        return remote(some, some, gb_send, gb_recv, dom=plane(i))

    @pl.loop(1, 8)
    def _(i):
        gw_copy(i).start()

    @pl.loop(1, 8)
    def _(i):
        gb_copy(i).start()

    wait_all(wcol.at[:, pl.ds(0, 7), :], gw_send, gw_recv)

    weights = [
        jnp.broadcast_to(wcol[j // 8, j % 8 : j % 8 + 1, :], (8, NY)) for j in range(COLS)
    ]

    @pl.loop(0, 3 * LZ)
    def _(b):
        for xt in range(CX // 8):
            own = slice(xt * 8 + FIRST, xt * 8 + FIRST + 8)
            total = [None, None]
            for j in range(COLS):
                term = weights[j] * panel[j * 3 * LZ + b, own, :]
                total[j % 2] = term if total[j % 2] is None else total[j % 2] + term
            corr_out[b, xt * 8 : xt * 8 + 8, :] = total[0] + total[1]

    wait_all(schur_v.at[:, pl.ds(0, 7)], gb_send, gb_recv)
    for half in range(2):
        for place in range(8):
            row = half * 8 + place
            for hi in range(8):
                schur_out[row : row + 1, hi * 256 : (hi + 1) * 256] = schur_v[
                    half, place, hi : hi + 1, :
                ]


def local(rhs, inv, trans, cell, well, coef, count, node, net, resid):
    f32 = jnp.float32
    any_space = pl.BlockSpec(memory_space=pl.ANY)
    vmem_space = pl.BlockSpec(memory_space=pltpu.VMEM)
    vmem = lambda *shape: pltpu.VMEM(shape, f32)
    dma = lambda *shape: pltpu.SemaphoreType.DMA(shape)
    corr, schur = pl.pallas_call(
        kernel,
        out_shape=(vmem(3 * LZ, CX, NY), vmem(COLS, NET)),
        in_specs=[any_space] * 10,
        out_specs=[vmem_space] * 2,
        scratch_shapes=[
            vmem(BLOCKS, ROWS, NY), vmem(BLOCKS, ROWS, NY), vmem(BLOCKS, ROWS, NY),
            vmem(9 * LZ, CX, NY), vmem(3 * LZ, CX, NY),
            vmem(LZ, ROWS, NY), vmem(LZ, ROWS, NY),
            vmem(LZ, CX, NY), vmem(LZ, CX, NY), vmem(LZ, CX, NY), vmem(LZ, CX, NY),
            vmem(9 * LZ, CX, NY),
            pltpu.VMEM((1, SLOTS), jnp.int32), pltpu.VMEM((1, SLOTS), jnp.int32),
            pltpu.SMEM((3, 1, SLOTS), f32), pltpu.SMEM((1, 1), jnp.int32),
            pltpu.VMEM((8, SLOTS), jnp.int32), pltpu.SMEM((8, SLOTS), jnp.int32),
            pltpu.VMEM((RES, WELLS), jnp.int32), vmem(2, 8, 256), vmem(8, 256),
            vmem(LZ * CX * PITCH, NY),
            vmem(4, 8, NY), vmem(8, 8, NY), vmem(32, 8, NY),
            pltpu.VMEM((256, NET), jnp.bfloat16),
            pltpu.VMEM((16 * PIECES, NET), jnp.bfloat16),
            vmem(2, 8, NY), vmem(2, 8, 8, 256),
            dma(10), dma(GROUPS),
            dma(SWEEPS, GROUPS, 2), dma(SWEEPS, GROUPS, 2), dma(2), dma(2),
            *[pltpu.SemaphoreType.DMA] * 10,
        ],
        compiler_params=pltpu.CompilerParams(
            collective_id=0, has_side_effects=True, vmem_limit_bytes=56 * 1024 * 1024
        ),
        cost_estimate=pl.CostEstimate(
            flops=120_000_000, bytes_accessed=8_500_000, transcendentals=0
        ),
    )(
        rhs.reshape(BLOCKS, CX, NY), inv.reshape(9 * LZ, CX, NY), trans.reshape(3 * LZ, CX, NY),
        cell, well, coef.transpose(1, 0, 2), count, node, net, resid.reshape(1, NET),
    )
    return corr.reshape(1, 3, LZ, CX, NY), schur


def solution(mesh):
    return jax.shard_map(
        local,
        mesh=mesh,
        in_specs=(
            P("res", None, None, "dom", None),
            P("res", None, None, None, "dom", None),
            P("res", None, None, "dom", None),
            P("res", "dom"),
            P("res", "dom"),
            P("res", None, "dom"),
            P("res", "dom"),
            P("res", None),
            P(),
            P(),
        ),
        out_specs=(P("res", None, None, "dom", None), P()),
        check_vma=False,
    )
```

```python
import math

import jax
import jax.numpy as jnp
from jax import lax
from jax.experimental import pallas as pl
from jax.experimental.pallas import tpu as pltpu
from jax.sharding import PartitionSpec as P

MESH = pl.DeviceIdType.MESH
SWEEPS = 4
COLS, LZ, CX, NY, NET, WELLS, SLOTS = 16, 8, 32, 128, 2048, 256, 256
RES, DOM = 8, 32
GROUPS = 4
GC = COLS // GROUPS
LOW, FIRST, LAST, HIGH = 7, 8, 39, 40
ROWS = 48
BLOCKS = COLS * 3 * LZ
GB = BLOCKS // GROUPS
PIECES = 3
PITCH = 3 * COLS + 1


def kernel(
    rhs, inv, trans, cell, well, coef, count, node, net, resid,
    corr_out, schur_out,
    q0, qa, qb, inv_v, trans_v, scale, edge, txm, txp, tym, typ, mats,
    cell_v, well_v, coef_s, count_s, slots_v, slots_s, nodes, net_v, resid_v,
    lines, rows, parts, sums, hot, lhs, wcol, schur_v,
    in_sem, rhs_sem, halo_send, halo_recv, edge_send, edge_recv,
    node_send, node_recv, rs_send, rs_recv, ga_send, ga_recv, gw_send, gw_recv, gb_send,
    gb_recv,
):
    f32 = jnp.float32
    res, dom = lax.axis_index("res"), lax.axis_index("dom")
    zlo, yc = dom // 8, dom % 8
    has_left, has_right = dom > 0, dom < DOM - 1

    def local(src, dst, i):
        return pltpu.make_async_copy(src, dst, in_sem.at[i])

    c_trans = local(trans, trans_v, 0)
    c_inv = local(inv, inv_v, 1)
    c_node = local(node, nodes.at[pl.ds(res, 1)], 2)
    c_small = [
        local(cell, cell_v, 3),
        local(well, well_v, 4),
        local(coef, coef_s, 5),
        local(count, count_s, 6),
    ]
    c_trans.start()
    c_node.start()
    c_inv.start()

    @pl.loop(0, COLS)
    def _(j):
        for c in range(3):
            pltpu.make_async_copy(
                rhs.at[pl.ds((c * COLS + j) * LZ, LZ)],
                q0.at[pl.ds((j * 3 + c) * LZ, LZ), pl.ds(FIRST, CX), :],
                rhs_sem.at[j // GC],
            ).start()

    for copy in c_small:
        copy.start()
    for hi in range(8):
        at = pl.ds(hi * 256, 256)
        for half in range(2):
            local(
                net.at[pl.ds(half * 8 + yc, 1), at], net_v.at[half, pl.ds(hi, 1), :], 7
            ).start()
        local(resid.at[:, at], resid_v.at[pl.ds(hi, 1), :], 8).start()

    barrier = pltpu.get_barrier_semaphore()

    def greet(**where):
        pl.semaphore_signal(barrier, inc=1, device_id=where, device_id_type=MESH)

    def plane(i):
        return zlo * 8 + lax.rem(yc + i, 8)

    def column(i):
        there = lax.rem(res * 4 + zlo + i, 32)
        return there // 4, lax.rem(there, 4) * 8 + yc

    greet(dom=lax.rem(dom + 1, DOM))
    greet(dom=lax.rem(dom + DOM - 1, DOM))
    for i in range(1, 8):
        greet(dom=plane(i))

    @pl.loop(1, 32)
    def _(i):
        r, d = column(i)
        greet(res=r, dom=d)

    lane = lax.broadcasted_iota(jnp.int32, (8, NY), 1)

    c_trans.wait()

    @pl.loop(0, CX // 8)
    def _(xt):
        at = pl.ds(xt * 8, 8)
        own = pl.ds(xt * 8 + FIRST, 8)
        e = jnp.ones((8, NY), f32)
        for l in range(LZ):
            if l:
                e = 1.0 / (trans_v[16 + l, at, :] * e)
            scale[l, own, :] = e
            edge[l, own, :] = trans_v[l, at, :] * e
            ty = trans_v[8 + l, at, :]
            tym[l, at, :] = jnp.where(lane == 0, 0.0, ty * e * pltpu.roll(e, 1, axis=1))
            typ[l, at, :] = jnp.where(lane == NY - 1, 0.0, e * pltpu.roll(ty * e, NY - 1, axis=1))

    c_node.wait()
    pl.semaphore_wait(barrier, 2 + 7 + 31)

    def remote(src, dst, send, recv, **where):
        return pltpu.make_async_remote_copy(
            src_ref=src, dst_ref=dst, send_sem=send, recv_sem=recv, device_id=where,
            device_id_type=MESH,
        )

    to_right = remote(
        scale.at[:, LAST, :], scale.at[:, LOW, :], edge_send.at[0], edge_recv.at[0],
        dom=jnp.minimum(dom + 1, DOM - 1),
    )
    to_left = remote(
        edge.at[:, FIRST, :], edge.at[:, HIGH, :], edge_send.at[1], edge_recv.at[1],
        dom=jnp.maximum(dom - 1, 0),
    )
    pl.when(has_right)(to_right.start)
    pl.when(has_left)(to_left.start)

    def node_copy(i):
        return remote(
            nodes.at[pl.ds(res, 1)], nodes.at[pl.ds(res, 1)], node_send, node_recv,
            res=lax.rem(res + i, RES),
        )

    @pl.loop(1, RES)
    def _(i):
        node_copy(i).start()

    def halo(buf, k, g, side):
        at = pl.ds(g * GB, GB)
        if side == 0:
            return remote(
                buf.at[at, LAST, :], buf.at[at, LOW, :], halo_send.at[k, g, 0],
                halo_recv.at[k, g, 0], dom=jnp.minimum(dom + 1, DOM - 1),
            )
        return remote(
            buf.at[at, FIRST, :], buf.at[at, HIGH, :], halo_send.at[k, g, 1],
            halo_recv.at[k, g, 1], dom=jnp.maximum(dom - 1, 0),
        )

    def halo_start(buf, k, g):
        pl.when(has_right)(halo(buf, k, g, 0).start)
        pl.when(has_left)(halo(buf, k, g, 1).start)

    def halo_wait(buf, k, g):
        @pl.when(has_right)
        def _():
            halo(buf, k, g, 0).wait_send()
            halo(buf, k, g, 1).wait_recv()

        @pl.when(has_left)
        def _():
            halo(buf, k, g, 1).wait_send()
            halo(buf, k, g, 0).wait_recv()

    for copy in c_small:
        copy.wait()
    at, to = cell_v[...], well_v[...]
    number = lax.broadcasted_iota(jnp.int32, (1, SLOTS), 1)
    numbers = (
        (at // NY) * PITCH, (to - at) & (NY - 1), jnp.where(number < count_s[0, 0], to, -1)
    )
    for i, values in enumerate(numbers):
        for half in range(2):
            slots_v[half * 8 + i : half * 8 + i + 1, :] = values[:, half * 128 : half * 128 + 128]
    c_slots = local(slots_v, slots_s, 9)
    c_slots.start()

    def clear(row, faces):
        faces[:, row : row + 1, :] = jnp.zeros((LZ, 1, NY), f32)

        @pl.loop(0, BLOCKS // 8)
        def _(b):
            for i in range(8):
                for buf in (q0, qa, qb):
                    buf[b * 8 + i, row : row + 1, :] = jnp.zeros((1, NY), f32)

    @pl.when(jnp.logical_not(has_left))
    def _():
        clear(LOW, scale)

    @pl.when(jnp.logical_not(has_right))
    def _():
        clear(HIGH, edge)

    c_inv.wait()

    @pl.loop(0, LZ)
    def _(l):
        for xt in range(CX // 8):
            at = slice(xt * 8, xt * 8 + 8)
            back = 1.0 / scale[l, xt * 8 + FIRST : xt * 8 + FIRST + 8, :]
            for n in range(9):
                mat = inv_v[n * LZ + l, at, :] * back
                inv_v[n * LZ + l, at, :] = mat
                mats[n * LZ + l, at, :] = mat * back

    @pl.loop(0, GROUPS)
    def _(g):
        whole = q0.at[pl.ds(g * GB, GB), pl.ds(FIRST, CX), :]
        pltpu.make_async_copy(whole, whole, rhs_sem.at[g]).wait()

        @pl.loop(0, LZ)
        def _(l):
            for xt in range(CX // 8):
                own = slice(xt * 8 + FIRST, xt * 8 + FIRST + 8)
                mat = [inv_v[n * LZ + l, xt * 8 : xt * 8 + 8, :] for n in range(9)]
                for j in range(GC):
                    base = (g * GC + j) * 3 * LZ + l
                    r = [q0[base + c * LZ, own, :] for c in range(3)]
                    for c in range(3):
                        q0[base + c * LZ, own, :] = (
                            mat[3 * c] * r[0] + mat[3 * c + 1] * r[1] + mat[3 * c + 2] * r[2]
                        )

        halo_start(q0, 0, g)

    pl.when(has_right)(to_right.wait_send)
    pl.when(has_left)(to_right.wait_recv)
    pl.when(has_left)(to_left.wait_send)
    pl.when(has_right)(to_left.wait_recv)

    @pl.loop(0, LZ)
    def _(l):
        txm[l] = edge[l, FIRST : FIRST + CX, :] * scale[l, LOW : LOW + CX, :]
        txp[l] = scale[l, FIRST : FIRST + CX, :] * edge[l, FIRST + 1 : FIRST + 1 + CX, :]

    def tile(src, dst, g, l, xt, below, above, last):
        at = slice(xt * 8, xt * 8 + 8)
        own = slice(xt * 8 + FIRST, xt * 8 + FIRST + 8)
        xlo = slice(xt * 8 + LOW, xt * 8 + LOW + 8)
        xhi = slice(xt * 8 + FIRST + 1, xt * 8 + FIRST + 9)
        am, ap, bm, bp = (ref[l, at, :] for ref in (txm, txp, tym, typ))
        mat = [mats[n * LZ + l, at, :] for n in range(9)]
        for j in range(GC):
            base = (g * GC + j) * 3 * LZ + l
            sums = []
            for c in range(3):
                b = base + c * LZ
                mid = src[b, own, :]
                s = am * src[b, xlo, :] + ap * src[b, xhi, :]
                s = s + (bm * pltpu.roll(mid, 1, axis=1) + bp * pltpu.roll(mid, NY - 1, axis=1))
                if below and above:
                    s = s + (src[b - 1, own, :] + src[b + 1, own, :])
                elif below:
                    s = s + src[b - 1, own, :]
                else:
                    s = s + src[b + 1, own, :]
                sums.append(s)
            for c in range(3):
                b = base + c * LZ
                out = (q0[b, own, :] + mat[3 * c] * sums[0]) + (
                    mat[3 * c + 1] * sums[1] + mat[3 * c + 2] * sums[2]
                )
                if last:
                    out = out * scale[l, own, :]
                    line = (l * CX + xt * 8) * PITCH + c * COLS + g * GC + j
                    lines[pl.ds(line, 8, stride=PITCH), :] = out
                dst[b, own, :] = out

    chain = [q0, qa, qb, qa, qb]
    for k in range(SWEEPS):
        src, dst, last = chain[k], chain[k + 1], k == SWEEPS - 1

        def part(g, columns, src=src, dst=dst, last=last):
            for l in range(LZ):
                for xt in columns:
                    tile(src, dst, g, l, xt, l > 0, l < LZ - 1, last)

        @pl.loop(0, GROUPS)
        def _(g):
            halo_wait(src, k, g)
            part(g, (0, CX // 8 - 1))
            if not last:
                halo_start(dst, k + 1, g)
            part(g, range(1, CX // 8 - 1))

    panel = chain[SWEEPS]

    c_slots.wait()
    lane = lax.broadcasted_iota(jnp.int32, (COLS, NY), 1)

    def slot(half, s, acc):
        base, turn, w = (slots_s[half * 8 + i, s] for i in range(3))
        line = None
        for c in range(3):
            part = coef_s[2 * c + half, 0, s] * lines[pl.ds(base + c * COLS, COLS), :]
            line = part if line is None else line + part
        line = pltpu.roll(line, turn, axis=1)
        return tuple(acc[h] + jnp.where(lane == w - h * NY, line, 0.0) for h in range(2))

    acc = (jnp.zeros((COLS, NY), f32),) * 2

    def some_slots(half, acc):
        for s in range(SLOTS // 2):
            acc = slot(half, s, acc)
        return acc

    acc = lax.fori_loop(0, 2, some_slots, acc)
    for h in range(2):
        for half in range(2):
            rows[2 * h + half] = acc[h][half * 8 : half * 8 + 8]

    def rs_copy(i):
        there = plane(i)
        return remote(
            rows.at[:, lax.rem(there, 8), :], parts.at[yc, pl.ds(0, 4), :], rs_send, rs_recv,
            dom=there,
        )

    @pl.loop(1, 8)
    def _(i):
        rs_copy(i).start()

    for z in range(4):
        parts[yc, z : z + 1, :] = rows[z, pl.ds(yc, 1), :]

    def wait_all(ref, *sems):
        for sem in sems:
            pltpu.make_async_copy(ref, ref, sem).wait()

    wait_all(nodes.at[pl.ds(0, RES - 1)], node_send, node_recv)

    sub = lax.broadcasted_iota(jnp.int32, (256, WELLS), 0)
    for r in range(RES):
        ids = nodes[r : r + 1, :]
        hot[:, r * WELLS : (r + 1) * WELLS] = jnp.where((ids & 255) == sub, 1.0, 0.0).astype(
            jnp.bfloat16
        )

    wait_all(parts.at[pl.ds(0, 7), pl.ds(0, 4), :], rs_send, rs_recv)

    total = parts[0, 0:4, :]
    for i in range(1, 8):
        total = total + parts[i, 0:4, :]
    mine = res * 4 + zlo
    sums[mine, 0:4, :] = total

    def ga_copy(i):
        r, d = column(i)
        some = sums.at[mine, pl.ds(0, 4), :]
        return remote(some, some, ga_send, ga_recv, res=r, dom=d)

    @pl.loop(1, 32)
    def _(i):
        ga_copy(i).start()

    wait_all(net_v, in_sem.at[7])
    wait_all(resid_v, in_sem.at[8])
    wait_all(sums.at[pl.ds(0, 31), pl.ds(0, 4), :], ga_send, ga_recv)

    sub8 = lax.broadcasted_iota(jnp.int32, (8, WELLS), 0)
    for r in range(RES):
        w = (sums[4 * r, 0:4, :] + sums[4 * r + 1, 0:4, :]) + (
            sums[4 * r + 2, 0:4, :] + sums[4 * r + 3, 0:4, :]
        )
        here = nodes[r : r + 1, :] // 256 == sub8
        for part in range(PIECES):
            now = w.astype(jnp.bfloat16).astype(f32)
            w = w - now
            tiles = []
            for half in range(2):
                line = jnp.concatenate([now[half : half + 1], now[half + 2 : half + 3]], axis=1)
                tiles.append(jnp.where(here, line, 0.0))
            lhs[part * 16 : part * 16 + 16, r * WELLS : (r + 1) * WELLS] = jnp.concatenate(
                tiles, axis=0
            ).astype(jnp.bfloat16)
    spread = lax.dot_general(
        lhs[...], hot[...], (((1,), (1,)), ((), ())), preferred_element_type=f32
    )
    spread = (spread[0:16] + spread[16:32]) + spread[32:48]
    for half in range(2):
        schur = net_v[half] - spread[half * 8 : half * 8 + 8]
        schur_v[half, yc] = schur
        weight = jnp.sum(schur * resid_v[...], axis=0, keepdims=True)
        weight = jnp.sum(weight, axis=1, keepdims=True) * (1.0 / math.sqrt(NET))
        wcol[half, pl.ds(yc, 1), :] = jnp.broadcast_to(weight, (1, NY))

    def gw_copy(i):
        some = wcol.at[:, yc, :]
        return remote(some, some, gw_send, gw_recv, dom=plane(i))

    def gb_copy(i):
        some = schur_v.at[:, yc]
        return remote(some, some, gb_send, gb_recv, dom=plane(i))

    @pl.loop(1, 8)
    def _(i):
        gw_copy(i).start()

    @pl.loop(1, 8)
    def _(i):
        gb_copy(i).start()

    wait_all(wcol.at[:, pl.ds(0, 7), :], gw_send, gw_recv)

    weights = [
        jnp.broadcast_to(wcol[j // 8, j % 8 : j % 8 + 1, :], (8, NY)) for j in range(COLS)
    ]

    @pl.loop(0, 3 * LZ)
    def _(b):
        for xt in range(CX // 8):
            own = slice(xt * 8 + FIRST, xt * 8 + FIRST + 8)
            total = [None, None]
            for j in range(COLS):
                term = weights[j] * panel[j * 3 * LZ + b, own, :]
                total[j % 2] = term if total[j % 2] is None else total[j % 2] + term
            corr_out[b, xt * 8 : xt * 8 + 8, :] = total[0] + total[1]

    wait_all(schur_v.at[:, pl.ds(0, 7)], gb_send, gb_recv)
    for half in range(2):
        for place in range(8):
            row = half * 8 + place
            for hi in range(8):
                schur_out[row : row + 1, hi * 256 : (hi + 1) * 256] = schur_v[
                    half, place, hi : hi + 1, :
                ]


def local(rhs, inv, trans, cell, well, coef, count, node, net, resid):
    f32 = jnp.float32
    any_space = pl.BlockSpec(memory_space=pl.ANY)
    vmem_space = pl.BlockSpec(memory_space=pltpu.VMEM)
    vmem = lambda *shape: pltpu.VMEM(shape, f32)
    dma = lambda *shape: pltpu.SemaphoreType.DMA(shape)
    corr, schur = pl.pallas_call(
        kernel,
        out_shape=(vmem(3 * LZ, CX, NY), vmem(COLS, NET)),
        in_specs=[any_space] * 10,
        out_specs=[vmem_space] * 2,
        scratch_shapes=[
            vmem(BLOCKS, ROWS, NY), vmem(BLOCKS, ROWS, NY), vmem(BLOCKS, ROWS, NY),
            vmem(9 * LZ, CX, NY), vmem(3 * LZ, CX, NY),
            vmem(LZ, ROWS, NY), vmem(LZ, ROWS, NY),
            vmem(LZ, CX, NY), vmem(LZ, CX, NY), vmem(LZ, CX, NY), vmem(LZ, CX, NY),
            vmem(9 * LZ, CX, NY),
            pltpu.VMEM((1, SLOTS), jnp.int32), pltpu.VMEM((1, SLOTS), jnp.int32),
            pltpu.SMEM((6, 1, SLOTS // 2), f32), pltpu.SMEM((1, 1), jnp.int32),
            pltpu.VMEM((16, SLOTS // 2), jnp.int32), pltpu.SMEM((16, SLOTS // 2), jnp.int32),
            pltpu.VMEM((RES, WELLS), jnp.int32), vmem(2, 8, 256), vmem(8, 256),
            vmem(LZ * CX * PITCH, NY),
            vmem(4, 8, NY), vmem(8, 8, NY), vmem(32, 8, NY),
            pltpu.VMEM((256, NET), jnp.bfloat16),
            pltpu.VMEM((16 * PIECES, NET), jnp.bfloat16),
            vmem(2, 8, NY), vmem(2, 8, 8, 256),
            dma(10), dma(GROUPS),
            dma(SWEEPS, GROUPS, 2), dma(SWEEPS, GROUPS, 2), dma(2), dma(2),
            *[pltpu.SemaphoreType.DMA] * 10,
        ],
        compiler_params=pltpu.CompilerParams(
            collective_id=0, has_side_effects=True, vmem_limit_bytes=56 * 1024 * 1024
        ),
        cost_estimate=pl.CostEstimate(
            flops=120_000_000, bytes_accessed=8_500_000, transcendentals=0
        ),
    )(
        rhs.reshape(BLOCKS, CX, NY), inv.reshape(9 * LZ, CX, NY), trans.reshape(3 * LZ, CX, NY),
        cell, well, coef.reshape(6, 1, SLOTS // 2), count, node, net, resid.reshape(1, NET),
    )
    return corr.reshape(1, 3, LZ, CX, NY), schur


def solution(mesh):
    return jax.shard_map(
        local,
        mesh=mesh,
        in_specs=(
            P("res", None, None, "dom", None),
            P("res", None, None, None, "dom", None),
            P("res", None, None, "dom", None),
            P("res", "dom"),
            P("res", "dom"),
            P("res", None, "dom"),
            P("res", "dom"),
            P("res", None),
            P(),
            P(),
        ),
        out_specs=(P("res", None, None, "dom", None), P()),
        check_vma=False,
    )
```

```python
import math

import jax
import jax.numpy as jnp
from jax import lax
from jax.experimental import pallas as pl
from jax.experimental.pallas import tpu as pltpu
from jax.sharding import PartitionSpec as P

MESH = pl.DeviceIdType.MESH
SWEEPS = 4
COLS, LZ, CX, NY, NET, WELLS, SLOTS = 16, 8, 32, 128, 2048, 256, 256
RES, DOM = 8, 32
GROUPS = 4
GC = COLS // GROUPS
LOW, FIRST, LAST, HIGH = 7, 8, 39, 40
ROWS = 48
BLOCKS = COLS * 3 * LZ
GB = BLOCKS // GROUPS
PIECES = 3
PITCH = 3 * COLS + 1


def kernel(
    rhs, inv, trans, cell, well, coef, count, node, net, resid,
    corr_out, schur_out,
    q0, qa, qb, inv_v, trans_v, scale, edge, txm, txp, tym, typ, mats,
    cell_v, well_v, coef_s, count_s, slots_v, slots_s, nodes, net_v, resid_v,
    lines, rows, parts, sums, hot, lhs, wcol, schur_v,
    in_sem, rhs_sem, halo_send, halo_recv, edge_send, edge_recv,
    node_send, node_recv, rs_send, rs_recv, ga_send, ga_recv, gw_send, gw_recv, gb_send,
    gb_recv,
):
    f32 = jnp.float32
    res, dom = lax.axis_index("res"), lax.axis_index("dom")
    zlo, yc = dom // 8, dom % 8
    has_left, has_right = dom > 0, dom < DOM - 1

    def local(src, dst, i):
        return pltpu.make_async_copy(src, dst, in_sem.at[i])

    c_trans = local(trans, trans_v, 0)
    c_inv = local(inv, inv_v, 1)
    c_node = local(node, nodes.at[pl.ds(res, 1)], 2)
    c_small = [
        local(cell, cell_v, 3),
        local(well, well_v, 4),
        local(coef, coef_s, 5),
        local(count, count_s, 6),
    ]
    c_trans.start()
    c_node.start()
    c_inv.start()

    @pl.loop(0, COLS)
    def _(j):
        for c in range(3):
            pltpu.make_async_copy(
                rhs.at[pl.ds((c * COLS + j) * LZ, LZ)],
                q0.at[pl.ds((j * 3 + c) * LZ, LZ), pl.ds(FIRST, CX), :],
                rhs_sem.at[j // GC],
            ).start()

    for copy in c_small:
        copy.start()
    for hi in range(8):
        at = pl.ds(hi * 256, 256)
        for half in range(2):
            local(
                net.at[pl.ds(half * 8 + yc, 1), at], net_v.at[half, pl.ds(hi, 1), :], 7
            ).start()
        local(resid.at[:, at], resid_v.at[pl.ds(hi, 1), :], 8).start()

    barrier = pltpu.get_barrier_semaphore()

    def greet(**where):
        pl.semaphore_signal(barrier, inc=1, device_id=where, device_id_type=MESH)

    def plane(i):
        return zlo * 8 + lax.rem(yc + i, 8)

    def column(i):
        there = lax.rem(res * 4 + zlo + i, 32)
        return there // 4, lax.rem(there, 4) * 8 + yc

    greet(dom=lax.rem(dom + 1, DOM))
    greet(dom=lax.rem(dom + DOM - 1, DOM))
    for i in range(1, 8):
        greet(dom=plane(i))

    @pl.loop(1, 32)
    def _(i):
        r, d = column(i)
        greet(res=r, dom=d)

    lane = lax.broadcasted_iota(jnp.int32, (8, NY), 1)

    c_trans.wait()

    @pl.loop(0, CX // 8)
    def _(xt):
        at = pl.ds(xt * 8, 8)
        own = pl.ds(xt * 8 + FIRST, 8)
        e = jnp.ones((8, NY), f32)
        for l in range(LZ):
            if l:
                e = 1.0 / (trans_v[16 + l, at, :] * e)
            scale[l, own, :] = e
            edge[l, own, :] = trans_v[l, at, :] * e
            ty = trans_v[8 + l, at, :]
            tym[l, at, :] = jnp.where(lane == 0, 0.0, ty * e * pltpu.roll(e, 1, axis=1))
            typ[l, at, :] = jnp.where(lane == NY - 1, 0.0, e * pltpu.roll(ty * e, NY - 1, axis=1))

    c_node.wait()
    pl.semaphore_wait(barrier, 2 + 7 + 31)

    def remote(src, dst, send, recv, **where):
        return pltpu.make_async_remote_copy(
            src_ref=src, dst_ref=dst, send_sem=send, recv_sem=recv, device_id=where,
            device_id_type=MESH,
        )

    to_right = remote(
        scale.at[:, LAST, :], scale.at[:, LOW, :], edge_send.at[0], edge_recv.at[0],
        dom=jnp.minimum(dom + 1, DOM - 1),
    )
    to_left = remote(
        edge.at[:, FIRST, :], edge.at[:, HIGH, :], edge_send.at[1], edge_recv.at[1],
        dom=jnp.maximum(dom - 1, 0),
    )
    pl.when(has_right)(to_right.start)
    pl.when(has_left)(to_left.start)

    def node_copy(i):
        return remote(
            nodes.at[pl.ds(res, 1)], nodes.at[pl.ds(res, 1)], node_send, node_recv,
            res=lax.rem(res + i, RES),
        )

    @pl.loop(1, RES)
    def _(i):
        node_copy(i).start()

    def halo(buf, k, g, side):
        at = pl.ds(g * GB, GB)
        if side == 0:
            return remote(
                buf.at[at, LAST, :], buf.at[at, LOW, :], halo_send.at[k, g, 0],
                halo_recv.at[k, g, 0], dom=jnp.minimum(dom + 1, DOM - 1),
            )
        return remote(
            buf.at[at, FIRST, :], buf.at[at, HIGH, :], halo_send.at[k, g, 1],
            halo_recv.at[k, g, 1], dom=jnp.maximum(dom - 1, 0),
        )

    def halo_start(buf, k, g):
        pl.when(has_right)(halo(buf, k, g, 0).start)
        pl.when(has_left)(halo(buf, k, g, 1).start)

    def halo_wait(buf, k, g):
        @pl.when(has_right)
        def _():
            halo(buf, k, g, 0).wait_send()
            halo(buf, k, g, 1).wait_recv()

        @pl.when(has_left)
        def _():
            halo(buf, k, g, 1).wait_send()
            halo(buf, k, g, 0).wait_recv()

    for copy in c_small:
        copy.wait()
    at, to = cell_v[...], well_v[...]
    number = lax.broadcasted_iota(jnp.int32, (1, SLOTS), 1)
    numbers = (
        (at // NY) * PITCH, (to - at) & (NY - 1), jnp.where(number < count_s[0, 0], to, -1)
    )
    for i, values in enumerate(numbers):
        for half in range(2):
            slots_v[half * 8 + i : half * 8 + i + 1, :] = values[:, half * 128 : half * 128 + 128]
    c_slots = local(slots_v, slots_s, 9)
    c_slots.start()

    def clear(row, faces):
        faces[:, row : row + 1, :] = jnp.zeros((LZ, 1, NY), f32)

        @pl.loop(0, BLOCKS // 8)
        def _(b):
            for i in range(8):
                for buf in (q0, qa, qb):
                    buf[b * 8 + i, row : row + 1, :] = jnp.zeros((1, NY), f32)

    @pl.when(jnp.logical_not(has_left))
    def _():
        clear(LOW, scale)

    @pl.when(jnp.logical_not(has_right))
    def _():
        clear(HIGH, edge)

    c_inv.wait()

    @pl.loop(0, LZ)
    def _(l):
        for xt in range(CX // 8):
            at = slice(xt * 8, xt * 8 + 8)
            back = 1.0 / scale[l, xt * 8 + FIRST : xt * 8 + FIRST + 8, :]
            for n in range(9):
                mat = inv_v[n * LZ + l, at, :] * back
                inv_v[n * LZ + l, at, :] = mat
                mats[n * LZ + l, at, :] = mat * back

    @pl.loop(0, GROUPS)
    def _(g):
        whole = q0.at[pl.ds(g * GB, GB), pl.ds(FIRST, CX), :]
        pltpu.make_async_copy(whole, whole, rhs_sem.at[g]).wait()

        @pl.loop(0, LZ)
        def _(l):
            for xt in range(CX // 8):
                own = slice(xt * 8 + FIRST, xt * 8 + FIRST + 8)
                mat = [inv_v[n * LZ + l, xt * 8 : xt * 8 + 8, :] for n in range(9)]
                for j in range(GC):
                    base = (g * GC + j) * 3 * LZ + l
                    r = [q0[base + c * LZ, own, :] for c in range(3)]
                    for c in range(3):
                        q0[base + c * LZ, own, :] = (
                            mat[3 * c] * r[0] + mat[3 * c + 1] * r[1] + mat[3 * c + 2] * r[2]
                        )

        halo_start(q0, 0, g)

    pl.when(has_right)(to_right.wait_send)
    pl.when(has_left)(to_right.wait_recv)
    pl.when(has_left)(to_left.wait_send)
    pl.when(has_right)(to_left.wait_recv)

    @pl.loop(0, LZ)
    def _(l):
        txm[l] = edge[l, FIRST : FIRST + CX, :] * scale[l, LOW : LOW + CX, :]
        txp[l] = scale[l, FIRST : FIRST + CX, :] * edge[l, FIRST + 1 : FIRST + 1 + CX, :]

    def tile(src, dst, g, l, xt, below, above, last):
        at = slice(xt * 8, xt * 8 + 8)
        own = slice(xt * 8 + FIRST, xt * 8 + FIRST + 8)
        xlo = slice(xt * 8 + LOW, xt * 8 + LOW + 8)
        xhi = slice(xt * 8 + FIRST + 1, xt * 8 + FIRST + 9)
        am, ap, bm, bp = (ref[l, at, :] for ref in (txm, txp, tym, typ))
        mat = [mats[n * LZ + l, at, :] for n in range(9)]
        for j in range(GC):
            base = (g * GC + j) * 3 * LZ + l
            sums = []
            for c in range(3):
                b = base + c * LZ
                mid = src[b, own, :]
                s = am * src[b, xlo, :] + ap * src[b, xhi, :]
                s = s + (bm * pltpu.roll(mid, 1, axis=1) + bp * pltpu.roll(mid, NY - 1, axis=1))
                if below and above:
                    s = s + (src[b - 1, own, :] + src[b + 1, own, :])
                elif below:
                    s = s + src[b - 1, own, :]
                else:
                    s = s + src[b + 1, own, :]
                sums.append(s)
            for c in range(3):
                b = base + c * LZ
                out = (q0[b, own, :] + mat[3 * c] * sums[0]) + (
                    mat[3 * c + 1] * sums[1] + mat[3 * c + 2] * sums[2]
                )
                if last:
                    out = out * scale[l, own, :]
                    line = (l * CX + xt * 8) * PITCH + c * COLS + g * GC + j
                    lines[pl.ds(line, 8, stride=PITCH), :] = out
                dst[b, own, :] = out

    chain = [q0, qa, qb, qa, qb]
    for k in range(SWEEPS):
        src, dst, last = chain[k], chain[k + 1], k == SWEEPS - 1

        def part(g, columns, src=src, dst=dst, last=last):
            for l in range(LZ):
                for xt in columns:
                    tile(src, dst, g, l, xt, l > 0, l < LZ - 1, last)

        if k == 0:

            @pl.loop(0, GROUPS)
            def _(g):
                part(g, range(1, CX // 8 - 1))

        @pl.loop(0, GROUPS)
        def _(g):
            if k:
                part(g, range(1, CX // 8 - 1))
            halo_wait(src, k, g)
            part(g, (0, CX // 8 - 1))
            if not last:
                halo_start(dst, k + 1, g)

    panel = chain[SWEEPS]

    c_slots.wait()
    lane = lax.broadcasted_iota(jnp.int32, (COLS, NY), 1)

    def slot(half, s, acc):
        base, turn, w = (slots_s[half * 8 + i, s] for i in range(3))
        line = None
        for c in range(3):
            part = coef_s[2 * c + half, 0, s] * lines[pl.ds(base + c * COLS, COLS), :]
            line = part if line is None else line + part
        line = pltpu.roll(line, turn, axis=1)
        return tuple(acc[h] + jnp.where(lane == w - h * NY, line, 0.0) for h in range(2))

    acc = (jnp.zeros((COLS, NY), f32),) * 2

    def some_slots(half, acc):
        for s in range(SLOTS // 2):
            acc = slot(half, s, acc)
        return acc

    acc = lax.fori_loop(0, 2, some_slots, acc)
    for h in range(2):
        for half in range(2):
            rows[2 * h + half] = acc[h][half * 8 : half * 8 + 8]

    def rs_copy(i):
        there = plane(i)
        return remote(
            rows.at[:, lax.rem(there, 8), :], parts.at[yc, pl.ds(0, 4), :], rs_send, rs_recv,
            dom=there,
        )

    @pl.loop(1, 8)
    def _(i):
        rs_copy(i).start()

    for z in range(4):
        parts[yc, z : z + 1, :] = rows[z, pl.ds(yc, 1), :]

    def wait_all(ref, *sems):
        for sem in sems:
            pltpu.make_async_copy(ref, ref, sem).wait()

    wait_all(nodes.at[pl.ds(0, RES - 1)], node_send, node_recv)

    sub = lax.broadcasted_iota(jnp.int32, (256, WELLS), 0)
    for r in range(RES):
        ids = nodes[r : r + 1, :]
        hot[:, r * WELLS : (r + 1) * WELLS] = jnp.where((ids & 255) == sub, 1.0, 0.0).astype(
            jnp.bfloat16
        )

    wait_all(parts.at[pl.ds(0, 7), pl.ds(0, 4), :], rs_send, rs_recv)

    total = parts[0, 0:4, :]
    for i in range(1, 8):
        total = total + parts[i, 0:4, :]
    mine = res * 4 + zlo
    sums[mine, 0:4, :] = total

    def ga_copy(i):
        r, d = column(i)
        some = sums.at[mine, pl.ds(0, 4), :]
        return remote(some, some, ga_send, ga_recv, res=r, dom=d)

    @pl.loop(1, 32)
    def _(i):
        ga_copy(i).start()

    wait_all(net_v, in_sem.at[7])
    wait_all(resid_v, in_sem.at[8])
    wait_all(sums.at[pl.ds(0, 31), pl.ds(0, 4), :], ga_send, ga_recv)

    sub8 = lax.broadcasted_iota(jnp.int32, (8, WELLS), 0)
    for r in range(RES):
        w = (sums[4 * r, 0:4, :] + sums[4 * r + 1, 0:4, :]) + (
            sums[4 * r + 2, 0:4, :] + sums[4 * r + 3, 0:4, :]
        )
        here = nodes[r : r + 1, :] // 256 == sub8
        for part in range(PIECES):
            now = w.astype(jnp.bfloat16).astype(f32)
            w = w - now
            tiles = []
            for half in range(2):
                line = jnp.concatenate([now[half : half + 1], now[half + 2 : half + 3]], axis=1)
                tiles.append(jnp.where(here, line, 0.0))
            lhs[part * 16 : part * 16 + 16, r * WELLS : (r + 1) * WELLS] = jnp.concatenate(
                tiles, axis=0
            ).astype(jnp.bfloat16)
    spread = lax.dot_general(
        lhs[...], hot[...], (((1,), (1,)), ((), ())), preferred_element_type=f32
    )
    spread = (spread[0:16] + spread[16:32]) + spread[32:48]
    for half in range(2):
        schur = net_v[half] - spread[half * 8 : half * 8 + 8]
        schur_v[half, yc] = schur
        weight = jnp.sum(schur * resid_v[...], axis=0, keepdims=True)
        weight = jnp.sum(weight, axis=1, keepdims=True) * (1.0 / math.sqrt(NET))
        wcol[half, pl.ds(yc, 1), :] = jnp.broadcast_to(weight, (1, NY))

    def gw_copy(i):
        some = wcol.at[:, yc, :]
        return remote(some, some, gw_send, gw_recv, dom=plane(i))

    def gb_copy(i):
        some = schur_v.at[:, yc]
        return remote(some, some, gb_send, gb_recv, dom=plane(i))

    @pl.loop(1, 8)
    def _(i):
        gw_copy(i).start()

    @pl.loop(1, 8)
    def _(i):
        gb_copy(i).start()

    wait_all(wcol.at[:, pl.ds(0, 7), :], gw_send, gw_recv)

    weights = [
        jnp.broadcast_to(wcol[j // 8, j % 8 : j % 8 + 1, :], (8, NY)) for j in range(COLS)
    ]

    @pl.loop(0, 3 * LZ)
    def _(b):
        for xt in range(CX // 8):
            own = slice(xt * 8 + FIRST, xt * 8 + FIRST + 8)
            total = [None, None]
            for j in range(COLS):
                term = weights[j] * panel[j * 3 * LZ + b, own, :]
                total[j % 2] = term if total[j % 2] is None else total[j % 2] + term
            corr_out[b, xt * 8 : xt * 8 + 8, :] = total[0] + total[1]

    wait_all(schur_v.at[:, pl.ds(0, 7)], gb_send, gb_recv)
    for half in range(2):
        for place in range(8):
            row = half * 8 + place
            for hi in range(8):
                schur_out[row : row + 1, hi * 256 : (hi + 1) * 256] = schur_v[
                    half, place, hi : hi + 1, :
                ]


def local(rhs, inv, trans, cell, well, coef, count, node, net, resid):
    f32 = jnp.float32
    any_space = pl.BlockSpec(memory_space=pl.ANY)
    vmem_space = pl.BlockSpec(memory_space=pltpu.VMEM)
    vmem = lambda *shape: pltpu.VMEM(shape, f32)
    dma = lambda *shape: pltpu.SemaphoreType.DMA(shape)
    corr, schur = pl.pallas_call(
        kernel,
        out_shape=(vmem(3 * LZ, CX, NY), vmem(COLS, NET)),
        in_specs=[any_space] * 10,
        out_specs=[vmem_space] * 2,
        scratch_shapes=[
            vmem(BLOCKS, ROWS, NY), vmem(BLOCKS, ROWS, NY), vmem(BLOCKS, ROWS, NY),
            vmem(9 * LZ, CX, NY), vmem(3 * LZ, CX, NY),
            vmem(LZ, ROWS, NY), vmem(LZ, ROWS, NY),
            vmem(LZ, CX, NY), vmem(LZ, CX, NY), vmem(LZ, CX, NY), vmem(LZ, CX, NY),
            vmem(9 * LZ, CX, NY),
            pltpu.VMEM((1, SLOTS), jnp.int32), pltpu.VMEM((1, SLOTS), jnp.int32),
            pltpu.SMEM((6, 1, SLOTS // 2), f32), pltpu.SMEM((1, 1), jnp.int32),
            pltpu.VMEM((16, SLOTS // 2), jnp.int32), pltpu.SMEM((16, SLOTS // 2), jnp.int32),
            pltpu.VMEM((RES, WELLS), jnp.int32), vmem(2, 8, 256), vmem(8, 256),
            vmem(LZ * CX * PITCH, NY),
            vmem(4, 8, NY), vmem(8, 8, NY), vmem(32, 8, NY),
            pltpu.VMEM((256, NET), jnp.bfloat16),
            pltpu.VMEM((16 * PIECES, NET), jnp.bfloat16),
            vmem(2, 8, NY), vmem(2, 8, 8, 256),
            dma(10), dma(GROUPS),
            dma(SWEEPS, GROUPS, 2), dma(SWEEPS, GROUPS, 2), dma(2), dma(2),
            *[pltpu.SemaphoreType.DMA] * 10,
        ],
        compiler_params=pltpu.CompilerParams(
            collective_id=0, has_side_effects=True, vmem_limit_bytes=56 * 1024 * 1024
        ),
        cost_estimate=pl.CostEstimate(
            flops=120_000_000, bytes_accessed=8_500_000, transcendentals=0
        ),
    )(
        rhs.reshape(BLOCKS, CX, NY), inv.reshape(9 * LZ, CX, NY), trans.reshape(3 * LZ, CX, NY),
        cell, well, coef.reshape(6, 1, SLOTS // 2), count, node, net, resid.reshape(1, NET),
    )
    return corr.reshape(1, 3, LZ, CX, NY), schur


def solution(mesh):
    return jax.shard_map(
        local,
        mesh=mesh,
        in_specs=(
            P("res", None, None, "dom", None),
            P("res", None, None, None, "dom", None),
            P("res", None, None, "dom", None),
            P("res", "dom"),
            P("res", "dom"),
            P("res", None, "dom"),
            P("res", "dom"),
            P("res", None),
            P(),
            P(),
        ),
        out_specs=(P("res", None, None, "dom", None), P()),
        check_vma=False,
    )
```
